256 devices in a mesh: col: 32 (over z_hi, x, core), row: 8 (over z_lo, y).
Axes of the slice: x: 4, y: 4, z: 8 (z_hi: 4, z_lo: 2; z = z_hi * 2 + z_lo), core: 2. Of those that a mesh axis runs over, the one named last changes fastest.
Arguments:
- row_vecs: bfloat16 [32768, 300], P(('row', 'col')), may hold values from -0.8984375 to 0.8984375
- row_bias: bfloat16 [32768], P(('row', 'col')), may hold values from -4 to 4
- col_vecs: bfloat16 [204800, 300], P(('col', 'row')), may hold values from -0.8984375 to 0.8984375
- col_bias: bfloat16 [204800], P(('col', 'row')), may hold values from -4 to 4
- row_block: int32 [8, 32, 128], P('row', 'col'), may hold values from 0 to 31, as said below
- col_block: int32 [8, 32, 128], P('row', 'col'), may hold values from 0 to 49
- counts: int32 [8, 32, 128, 128, 128], P('row', 'col'), may hold values from 0 to 512, as said below
- block_totals: int32 [8, 32], replicated, may hold values from 42 to 128, as said below
Outputs:
- grad_rows: float32 [32768, 300], P(('row', 'col'))
- grad_row_bias: float32 [32768], P(('row', 'col'))
- grad_cols: float32 [204800, 300], P(('col', 'row'))
- grad_col_bias: float32 [204800], P(('col', 'row'))
The draws below stay inside these ranges and needn't reach their ends.
Inputs may be any that keep to these rules, and one draw needn't show every extreme that they name: On each device the pairs (row_block, col_block) of its 128 slots are distinct. Slots at or after a device's block total may hold any counts. `block_totals`: some device has exactly 128 live slots and some other device exactly 42.
All inputs are finite; a program needn't handle non-finite values.
Results may differ from the reference program's by a relative error of at most 0.0028.
Values may be sent and summed in bfloat16 or wider, within the bound.
A program may use at most 192 MiB of HBM per device.

```python
import jax
import jax.numpy as jnp
from jax import lax

D = 300
BLK = 128
COLS_DEV = 6400
ROWS_DEV = 4096
CAP = 128
ROW_TILES = 32
COL_TILES = 50
ROWS = 32768
VOCAB = 204800
N_COL = 32
N_ROW = 8


def slot_cells(key):
    device_keys = jax.random.split(key, N_ROW * N_COL)

    def one_device(device_key):
        return jax.random.permutation(device_key, ROW_TILES * COL_TILES)[:CAP]
    return jax.vmap(one_device)(device_keys).reshape(N_ROW, N_COL, CAP).astype(jnp.int32)


def draw_row_block(key, part):
    cells = slot_cells(key)
    return cells // COL_TILES


def draw_col_block(key, part):
    cells = slot_cells(key)
    return cells % COL_TILES


def draw_counts(key, part):
    key = jax.random.fold_in(key, 4)
    shape = (N_ROW, N_COL, CAP, BLK, BLK)
    raw_bits = jax.random.randint(key, shape, 0, 5 * 10 * 512)
    present = raw_bits % 5 >= 2
    levels = raw_bits // 5 % 10
    spread = raw_bits // 50 % 512
    values = 1 + spread % jnp.left_shift(jnp.ones_like(levels), levels)
    return jnp.where(present, values, 0).astype(jnp.int32)


def draw_block_totals(key, part):
    key = jax.random.fold_in(key, 5)
    total_key, chosen_key, offset_key = jax.random.split(key, 3)
    device_count = N_ROW * N_COL
    lowest = CAP // 3
    totals = jax.random.randint(total_key, (device_count,), lowest, CAP + 1)
    chosen = jax.random.randint(chosen_key, (), 0, device_count)
    offset = jax.random.randint(offset_key, (), 0, device_count - 1)
    second = (chosen + 1 + offset) % device_count
    places = jnp.arange(device_count)
    totals = jnp.where(places == chosen, CAP, totals)
    totals = jnp.where(places == second, lowest, totals)
    return totals.reshape(N_ROW, N_COL).astype(jnp.int32)


def shard_levels(rng, extent, cuts, smallest, high):
    factor_of = 1.0
    for position, blocks in cuts:
        heights = jax.random.uniform(jax.random.fold_in(jax.random.fold_in(rng, 6), position), (blocks,), jnp.float32, smallest / len(cuts), high / len(cuts))
        factor_of = factor_of * jnp.repeat(jnp.exp(heights), extent[position] // blocks).reshape((-1,) + (1,) * (len(extent) - 1 - position))
    return factor_of


def noise(rng, dims, deviation, limit, shards=(), held_as=jnp.bfloat16):
    result = deviation * jax.random.normal(rng, dims, jnp.float32)
    if shards:
        result = result * shard_levels(rng, dims, shards, -0.22, 0.18)
    return jnp.clip(result, -limit, limit).astype(held_as)


def setup_inputs(seed: int = 0) -> dict:
    arg_keys = jax.random.split(jax.random.key(seed), 9)
    row_vecs = noise(arg_keys[0], (ROWS, D), 0.15, 0.8984375, ((0, 256),))
    row_bias = noise(arg_keys[1], (ROWS,), 1.0, 4.0, ((0, 256),))
    col_vecs = noise(arg_keys[2], (VOCAB, D), 0.15, 0.8984375, ((0, 256),))
    col_bias = noise(arg_keys[3], (VOCAB,), 1.0, 4.0, ((0, 256),))
    row_block = draw_row_block(jax.random.fold_in(arg_keys[8], 71), 0)
    col_block = draw_col_block(jax.random.fold_in(arg_keys[8], 71), 0)
    counts = draw_counts(jax.random.fold_in(arg_keys[8], 71), 0)
    block_totals = draw_block_totals(jax.random.fold_in(arg_keys[8], 71), 0)
    return {"row_vecs": row_vecs, "row_bias": row_bias, "col_vecs": col_vecs, "col_bias": col_bias, "row_block": row_block, "col_block": col_block, "counts": counts, "block_totals": block_totals}


def reference(row_vecs, row_bias, col_vecs, col_bias, row_block, col_block, counts, block_totals):
    def visit(device_flat, running):
        grad_rows, grad_row_bias, grad_cols, grad_col_bias = running
        row_index = (device_flat // N_COL).astype(jnp.int32)
        col_index = (device_flat % N_COL).astype(jnp.int32)
        row_start = (row_index * ROWS_DEV).astype(jnp.int32)
        col_start = (col_index * COLS_DEV).astype(jnp.int32)
        row_tiles = lax.dynamic_slice_in_dim(row_vecs, row_start, ROWS_DEV, 0).reshape(ROW_TILES, BLK, D)
        row_shifts = lax.dynamic_slice_in_dim(row_bias, row_start, ROWS_DEV, 0).reshape(ROW_TILES, BLK)
        col_tiles = lax.dynamic_slice_in_dim(col_vecs, col_start, COLS_DEV, 0).reshape(COL_TILES, BLK, D)
        col_shifts = lax.dynamic_slice_in_dim(col_bias, col_start, COLS_DEV, 0).reshape(COL_TILES, BLK)
        row_ids = row_block[row_index, col_index]
        col_ids = col_block[row_index, col_index]
        tiles_here = counts[row_index, col_index]
        live_count = block_totals[row_index, col_index]
        live_mask = (jnp.arange(CAP, dtype=jnp.int32) < live_count).astype(jnp.float32)
        row_part = row_tiles[row_ids].astype(jnp.float32)
        col_part = col_tiles[col_ids].astype(jnp.float32)
        counts_real = tiles_here.astype(jnp.float32)
        scores = jnp.einsum("nid,njd->nij", row_part, col_part, precision=lax.Precision.HIGHEST)
        residual = scores + row_shifts[row_ids].astype(jnp.float32)[:, :, None] + col_shifts[col_ids].astype(jnp.float32)[:, None, :] - jnp.log(jnp.maximum(counts_real, 1.0))
        weights = jnp.minimum(1.0, jnp.power(counts_real / 100.0, 0.75))
        terms = 2.0 * weights * residual * live_mask[:, None, None]
        rounded = lax.optimization_barrier(terms.astype(jnp.bfloat16)).astype(jnp.float32)
        tile_rows = jnp.einsum("nij,njd->nid", rounded, col_part, precision=lax.Precision.HIGHEST)
        tile_cols = jnp.einsum("nij,nid->njd", rounded, row_part, precision=lax.Precision.HIGHEST)
        part_rows = jnp.zeros((ROW_TILES, BLK, D), jnp.float32).at[row_ids].add(tile_rows).reshape(ROWS_DEV, D)
        part_row_bias = jnp.zeros((ROW_TILES, BLK), jnp.float32).at[row_ids].add(jnp.sum(terms, axis=2)).reshape(ROWS_DEV)
        part_cols = jnp.zeros((COL_TILES, BLK, D), jnp.float32).at[col_ids].add(tile_cols).reshape(COLS_DEV, D)
        part_col_bias = jnp.zeros((COL_TILES, BLK), jnp.float32).at[col_ids].add(jnp.sum(terms, axis=1)).reshape(COLS_DEV)
        grad_rows = lax.dynamic_update_slice_in_dim(grad_rows, lax.dynamic_slice_in_dim(grad_rows, row_start, ROWS_DEV, 0) + part_rows, row_start, 0)
        grad_row_bias = lax.dynamic_update_slice_in_dim(grad_row_bias, lax.dynamic_slice_in_dim(grad_row_bias, row_start, ROWS_DEV, 0) + part_row_bias, row_start, 0)
        grad_cols = lax.dynamic_update_slice_in_dim(grad_cols, lax.dynamic_slice_in_dim(grad_cols, col_start, COLS_DEV, 0) + part_cols, col_start, 0)
        grad_col_bias = lax.dynamic_update_slice_in_dim(grad_col_bias, lax.dynamic_slice_in_dim(grad_col_bias, col_start, COLS_DEV, 0) + part_col_bias, col_start, 0)
        return (grad_rows, grad_row_bias, grad_cols, grad_col_bias)

    initial = (jnp.zeros((ROWS, D), jnp.float32), jnp.zeros((ROWS,), jnp.float32), jnp.zeros((VOCAB, D), jnp.float32), jnp.zeros((VOCAB,), jnp.float32))
    grad_rows, grad_row_bias, grad_cols, grad_col_bias = lax.fori_loop(0, N_ROW * N_COL, visit, initial)
    return (grad_rows, grad_row_bias, grad_cols, grad_col_bias)
```

```python
import functools

import jax
import jax.numpy as jnp
from jax import lax
from jax.experimental import pallas as pl
from jax.experimental.pallas import tpu as pltpu
from jax.sharding import PartitionSpec as P

MESH = pl.DeviceIdType.MESH
ANY = pl.BlockSpec(memory_space=pl.ANY)
IN_VMEM = pl.BlockSpec(memory_space=pltpu.VMEM)
F32, BF16 = jnp.float32, jnp.bfloat16

D = 300
DP = 304
L = 128
SHARD = 800
FULL = SHARD // L
QR = 80
PACK = FULL * DP + QR
HALF = 960
RHALF = 160
SHARDS = 8
ROW_TILES = 32
COL_TILES = 50
CAP = 128
GROUP = 8
VMEM_LIMIT = 56 * 1024 * 1024


def place():
    row, col = lax.axis_index("row"), lax.axis_index("col")
    y, zl = row % 4, row // 4
    core, x, zh = col % 2, (col // 2) % 4, col // 8
    return y, zl, core, x, zh


def row_of(y, zl):
    return zl * 4 + y


def col_of(core, x, zh):
    return (zh * 4 + x) * 2 + core


class Ring:
    def __init__(self, send, recv):
        self.send, self.recv = send, recv
        self.y, self.zl, self.core, self.x, self.zh = place()
        y, zl, core, x, zh = self.y, self.zl, self.core, self.x, self.zh
        row, col = row_of(y, zl), col_of(core, x, zh)
        self.near = {
            "y+": (row_of((y + 1) % 4, zl), col),
            "y-": (row_of((y + 3) % 4, zl), col),
            "zl": (row_of(y, 1 - zl), col),
            "x+": (row, col_of(core, (x + 1) % 4, zh)),
            "x-": (row, col_of(core, (x + 3) % 4, zh)),
            "zh+": (row, col_of(core, x, (zh + 1) % 4)),
            "zh-": (row, col_of(core, x, (zh + 3) % 4)),
            "core": (row, col_of(1 - core, x, zh)),
        }
        self.started = []

    def greet(self):
        barrier = pltpu.get_barrier_semaphore()
        for row, col in self.near.values():
            pl.semaphore_signal(barrier, inc=1, device_id={"row": row, "col": col}, device_id_type=MESH)
        return barrier

    def meet(self, barrier):
        pl.semaphore_wait(barrier, len(self.near))

    def copy(self, k, to, src, dst):
        row, col = self.near[to]
        out = pltpu.make_async_remote_copy(
            src_ref=src,
            dst_ref=dst,
            send_sem=self.send.at[k],
            recv_sem=self.recv.at[k],
            device_id={"row": row, "col": col},
            device_id_type=MESH,
        )
        out.start()
        self.started.append(out)
        return out

    def finish(self):
        for out in self.started:
            out.wait_send()


def gather_kernel(ct_ref, rt_ref, gc_ref, gr_ref, wc, send, recv, local):
    ring = Ring(send, recv)
    y, zl, core, x, zh = ring.y, ring.zl, ring.core, ring.x, ring.zh
    barrier = ring.greet()
    for t in range(FULL):
        wc[t * DP : (t + 1) * DP] = ct_ref[0:DP, t * L : (t + 1) * L]
    tail = ct_ref[0:QR, FULL * L : (FULL + 1) * L].astype(F32)
    for q in range(1, 4):
        part = ct_ref[q * QR : (q + 1) * QR, FULL * L : (FULL + 1) * L].astype(F32)
        tail = tail + pltpu.roll(part, 32 * q, 1)
    wc[FULL * DP : PACK] = tail.astype(BF16)
    mine = row_of(y, zl)
    other = row_of(y, 1 - zl)
    up, down, far = (y + 1) % 4, (y + 3) % 4, (y + 2) % 4
    own_c = pltpu.make_async_copy(wc, gc_ref.at[mine], local.at[0])
    own_r = pltpu.make_async_copy(rt_ref, gr_ref.at[core, x, zh], local.at[1])
    own_c.start()
    own_r.start()
    ring.meet(barrier)
    c_y0 = ring.copy(0, "y+", wc, gc_ref.at[mine])
    c_y1 = ring.copy(1, "y-", wc, gc_ref.at[mine])
    r_z0 = ring.copy(2, "zh+", rt_ref, gr_ref.at[core, x, zh])
    r_z1 = ring.copy(3, "zh-", rt_ref, gr_ref.at[core, x, zh])
    c_z = ring.copy(4, "zl", wc, gc_ref.at[mine])

    lo, hi = pl.ds(0, RHALF), pl.ds(RHALF, DP - RHALF)
    r_z0.wait_recv()
    part = gr_ref.at[core, x, (zh + 3) % 4, lo]
    r_z2 = ring.copy(5, "zh+", part, part)
    r_z1.wait_recv()
    part = gr_ref.at[core, x, (zh + 1) % 4, hi]
    r_z3 = ring.copy(6, "zh-", part, part)
    r_z2.wait_recv()
    r_z3.wait_recv()
    own_r.wait()
    part = gr_ref.at[core, x]
    r_x0 = ring.copy(7, "x+", part, part)
    r_x1 = ring.copy(8, "x-", part, part)
    r_c0 = ring.copy(9, "core", part, part)

    lo, hi = pl.ds(0, HALF), pl.ds(HALF, PACK - HALF)
    c_y0.wait_recv()
    part = gc_ref.at[row_of(down, zl), lo]
    c_y2 = ring.copy(10, "y+", part, part)
    c_y1.wait_recv()
    part = gc_ref.at[row_of(up, zl), hi]
    c_y3 = ring.copy(11, "y-", part, part)
    c_z.wait_recv()
    part = gc_ref.at[other]
    c_y4 = ring.copy(12, "y+", part, part)
    c_y5 = ring.copy(13, "y-", part, part)

    r_x0.wait_recv()
    part = gr_ref.at[core, (x + 3) % 4, pl.ds(0, 2)]
    r_x2 = ring.copy(14, "x+", part, part)
    part = gr_ref.at[core, (x + 3) % 4]
    r_c1 = ring.copy(15, "core", part, part)
    r_x1.wait_recv()
    part = gr_ref.at[core, (x + 1) % 4, pl.ds(2, 2)]
    r_x3 = ring.copy(16, "x-", part, part)
    part = gr_ref.at[core, (x + 1) % 4]
    r_c2 = ring.copy(17, "core", part, part)
    r_x2.wait_recv()
    r_x3.wait_recv()
    part = gr_ref.at[core, (x + 2) % 4]
    r_c3 = ring.copy(18, "core", part, part)

    c_y2.wait_recv()
    c_y3.wait_recv()
    part = gc_ref.at[row_of(far, zl)]
    c_z1 = ring.copy(19, "zl", part, part)

    for done in (r_c0, r_c1, r_c2, r_c3, c_y4, c_y5, c_z1):
        done.wait_recv()
    ring.finish()
    own_c.wait()


def gather(ct, rt):
    return pl.pallas_call(
        gather_kernel,
        out_shape=(
            jax.ShapeDtypeStruct((SHARDS, PACK, L), BF16),
            jax.ShapeDtypeStruct((2, 4, 4, DP, L), BF16),
        ),
        in_specs=[IN_VMEM, IN_VMEM],
        out_specs=(ANY, ANY),
        scratch_shapes=[
            pltpu.VMEM((PACK, L), BF16),
            pltpu.SemaphoreType.DMA((20,)),
            pltpu.SemaphoreType.DMA((20,)),
            pltpu.SemaphoreType.DMA((2,)),
        ],
        compiler_params=pltpu.CompilerParams(
            collective_id=0, has_side_effects=True, vmem_limit_bytes=VMEM_LIMIT
        ),
        name="gather",
    )(ct, rt)


def shards_to_tiles(packed, tiles):
    lane = lax.broadcasted_iota(jnp.int32, (DP, L), 1)
    at, carry = 0, None
    for s in range(SHARDS):
        shift = (32 * s) % L
        for t in range(FULL):
            cur = packed[s, t * DP : (t + 1) * DP].astype(F32)
            if shift:
                cur = pltpu.roll(cur, shift, 1)
                tiles[at] = jnp.where(lane < shift, carry, cur).astype(BF16)
            else:
                tiles[at] = cur.astype(BF16)
            at, carry = at + 1, cur
        tail = packed[s, FULL * DP : PACK].astype(F32)
        parts = [pltpu.roll(tail, (shift - 32 * q) % L, 1) if (shift - 32 * q) % L else tail for q in range(4)]
        cur = jnp.concatenate(parts, axis=0)[:DP]
        if shift:
            cur = jnp.where(lane < shift, carry, cur)
        if shift + 32 == L:
            tiles[at] = cur.astype(BF16)
            at, carry = at + 1, None
        else:
            carry = cur


def tiles_to_shards(tiles, packed):
    lane = lax.broadcasted_iota(jnp.int32, (DP, L), 1)
    lane_q = lax.broadcasted_iota(jnp.int32, (QR, L), 1)
    for s in range(SHARDS):
        shift = (32 * s) % L
        base = (SHARD * s) // L
        cur = tiles[base]
        if shift:
            cur = pltpu.roll(cur, L - shift, 1)
        for t in range(FULL):
            nxt = tiles[base + t + 1]
            if shift:
                nxt = pltpu.roll(nxt, L - shift, 1)
                packed[s, t * DP : (t + 1) * DP] = jnp.where(lane < L - shift, cur, nxt).astype(BF16)
            else:
                packed[s, t * DP : (t + 1) * DP] = cur.astype(BF16)
            cur = nxt
        cur = jnp.concatenate([cur, jnp.zeros((4 * QR - DP, L), F32)], axis=0)
        tail = cur[:QR]
        for q in range(1, 4):
            tail = jnp.where(lane_q < 32 * q, tail, pltpu.roll(cur[q * QR : (q + 1) * QR], 32 * q, 1))
        packed[s, FULL * DP : PACK] = tail.astype(BF16)


LOG2_100 = 6.643856189774724
LN2 = 0.6931471805599453


def blocks_kernel(total_ref, rid_ref, cid_ref, counts_ref, gc_ref, gr_ref, pc_ref, pr_ref,
                  counts, packed, rt, rn, ct, acc_c, acc_r, sems, count_sems):
    row, col = lax.axis_index("row"), lax.axis_index("col")
    total = total_ref[row, col]
    groups = (total + GROUP - 1) // GROUP
    load_r = pltpu.make_async_copy(gr_ref, rt, sems.at[0])
    load_c = pltpu.make_async_copy(gc_ref, packed, sems.at[1])
    load_r.start()
    load_c.start()

    def load(g):
        part = pl.ds(g * GROUP, GROUP)
        return pltpu.make_async_copy(counts_ref.at[part], counts.at[part], count_sems.at[g])

    @pl.loop(0, groups)
    def _(g):
        load(g).start()

    @pl.loop(0, COL_TILES)
    def _(i):
        acc_c[i] = jnp.zeros((DP, L), F32)

    @pl.loop(0, ROW_TILES)
    def _(i):
        acc_r[i] = jnp.zeros((DP, L), F32)

    load_r.wait()

    @pl.loop(0, ROW_TILES)
    def _(i):
        rn[i] = rt[i].astype(F32).T.astype(BF16)

    load_c.wait()
    shards_to_tiles(packed, ct)

    @pl.loop(0, groups)
    def _(g):
        load(g).wait()
        terms, rids, cids = [], [], []
        for k in range(GROUP):
            n = g * GROUP + k
            rid, cid = rid_ref[n], cid_ref[n]
            rids.append(rid)
            cids.append(cid)
            scores = jnp.dot(rn[rid], ct[cid], preferred_element_type=F32)
            x = counts[n]
            least = jnp.where(n < total, 0, jnp.int32(2**31 - 1))
            log2x = jnp.log2(jnp.maximum(x.astype(F32), 1.0))
            weight2 = jnp.exp2(jnp.minimum(0.75 * log2x + (1.0 - 0.75 * LOG2_100), 1.0))
            term = weight2 * (scores - LN2 * log2x)
            terms.append(jnp.where(x > least, term, 0.0).astype(BF16))
        for k in range(GROUP):
            acc_c[cids[k]] += jnp.dot(rt[rids[k]], terms[k], preferred_element_type=F32)
            acc_r[rids[k]] += lax.dot_general(
                ct[cids[k]], terms[k], (((1,), (1,)), ((), ())), preferred_element_type=F32
            )

    tiles_to_shards(acc_c, packed)
    out_c = pltpu.make_async_copy(packed, pc_ref, sems.at[0])
    out_r = pltpu.make_async_copy(acc_r, pr_ref, sems.at[1])
    out_c.start()
    out_r.start()
    out_c.wait()
    out_r.wait()


def blocks(totals, rid, cid, counts, gc, gr):
    smem = pl.BlockSpec(memory_space=pltpu.SMEM)
    return pl.pallas_call(
        blocks_kernel,
        out_shape=(
            jax.ShapeDtypeStruct((SHARDS, PACK, L), BF16),
            jax.ShapeDtypeStruct((ROW_TILES, DP, L), F32),
        ),
        in_specs=[smem, smem, smem, ANY, ANY, ANY],
        out_specs=(ANY, ANY),
        scratch_shapes=[
            pltpu.VMEM((CAP, L, L), jnp.int32),
            pltpu.VMEM((SHARDS, PACK, L), BF16),
            pltpu.VMEM((ROW_TILES, DP, L), BF16),
            pltpu.VMEM((ROW_TILES, L, DP), BF16),
            pltpu.VMEM((COL_TILES, DP, L), BF16),
            pltpu.VMEM((COL_TILES, DP, L), F32),
            pltpu.VMEM((ROW_TILES, DP, L), F32),
            pltpu.SemaphoreType.DMA((2,)),
            pltpu.SemaphoreType.DMA((CAP // GROUP,)),
        ],
        compiler_params=pltpu.CompilerParams(vmem_limit_bytes=VMEM_LIMIT),
        name="blocks",
    )(totals, rid, cid, counts, gc, gr)


def reduce_kernel(pc_ref, pr_ref, oc_ref, obc_ref, or_ref, obr_ref,
                  pc, pr, got_c, half_c, put_c, got_core, got_x, put_x, half_x, half_z, got_z, put_z, u,
                  send, recv, local):
    ring = Ring(send, recv)
    y, zl, core, x, zh = ring.y, ring.zl, ring.core, ring.x, ring.zh
    zo = 1 - zl
    barrier = ring.greet()
    up, down, far = (y + 1) % 4, (y + 3) % 4, (y + 2) % 4
    xu, xd, xf = (x + 1) % 4, (x + 3) % 4, (x + 2) % 4
    zu, zd, zf = (zh + 1) % 4, (zh + 3) % 4, (zh + 2) % 4
    wanted = (row_of(far, zl), row_of(up, zl), row_of(down, zl), row_of(y, zo), row_of(y, zl))
    loads = [pltpu.make_async_copy(pc_ref.at[w], pc.at[i], local.at[i]) for i, w in enumerate(wanted)]
    load_r = pltpu.make_async_copy(pr_ref.at[core], pr, local.at[5])
    loads[0].start()
    load_r.start()
    for k in range(1, 5):
        loads[k].start()
    ring.meet(barrier)
    a_z = ring.copy(0, "zl", pc_ref.at[row_of(far, zo)], got_c.at[0])
    a_y0 = ring.copy(1, "y+", pc_ref.at[row_of(up, zo)], got_c.at[1])
    a_y1 = ring.copy(2, "y-", pc_ref.at[row_of(down, zo)], got_c.at[2])
    b_c = [
        ring.copy(3 + k, "core", pr_ref.at[1 - core, w], got_core.at[k])
        for k, w in enumerate((xf, xu, xd, x))
    ]
    load_r.wait()

    b_c[0].wait_recv()
    for z in range(4):
        put_x[0, z] = (pr[xf, z] + got_core[0, z]).astype(BF16)
    b_x0 = ring.copy(7, "x+", put_x.at[0, pl.ds(0, 2)], half_x.at[0])
    b_x1 = ring.copy(8, "x-", put_x.at[0, pl.ds(2, 2)], half_x.at[1])

    b_c[1].wait_recv()
    b_x0.wait_recv()
    for z in range(4):
        total = pr[xu, z] + got_core[1, z]
        if z < 2:
            total = total + half_x[0, z].astype(F32)
        put_x[1, z] = total.astype(BF16)
    b_x2 = ring.copy(9, "x+", put_x.at[1], got_x.at[0])
    b_c[2].wait_recv()
    b_x1.wait_recv()
    for z in range(4):
        total = pr[xd, z] + got_core[2, z]
        if z >= 2:
            total = total + half_x[1, z - 2].astype(F32)
        put_x[2, z] = total.astype(BF16)
    b_x3 = ring.copy(10, "x-", put_x.at[2], got_x.at[1])

    loads[0].wait()
    a_z.wait_recv()
    put_c[0] = (pc[0].astype(F32) + got_c[0].astype(F32)).astype(BF16)
    lo, hi = pl.ds(0, HALF), pl.ds(HALF, PACK - HALF)
    a_y2 = ring.copy(11, "y+", put_c.at[0, lo], half_c.at[lo])
    a_y3 = ring.copy(12, "y-", put_c.at[0, hi], half_c.at[hi])

    loads[3].wait()
    a_y0.wait_recv()
    a_y1.wait_recv()
    put_c[1] = (pc[3].astype(F32) + got_c[1].astype(F32) + got_c[2].astype(F32)).astype(BF16)
    a_z1 = ring.copy(13, "zl", put_c.at[1], got_c.at[3])

    b_c[3].wait_recv()
    b_x2.wait_recv()
    b_x3.wait_recv()
    for z in range(4):
        u[z] = pr[x, z] + got_core[3, z] + got_x[0, z].astype(F32) + got_x[1, z].astype(F32)
    put_z[0] = u[zf].astype(BF16)
    rlo, rhi = pl.ds(0, RHALF), pl.ds(RHALF, DP - RHALF)
    b_z0 = ring.copy(14, "zh+", put_z.at[0, rlo], half_z.at[rlo])
    b_z1 = ring.copy(15, "zh-", put_z.at[0, rhi], half_z.at[rhi])

    loads[1].wait()
    a_y2.wait_recv()
    put_c[2, 0:HALF] = (pc[1, 0:HALF].astype(F32) + half_c[0:HALF].astype(F32)).astype(BF16)
    put_c[2, HALF:PACK] = pc[1, HALF:PACK]
    a_y4 = ring.copy(16, "y+", put_c.at[2], got_c.at[4])
    loads[2].wait()
    a_y3.wait_recv()
    put_c[3, 0:HALF] = pc[2, 0:HALF]
    put_c[3, HALF:PACK] = (pc[2, HALF:PACK].astype(F32) + half_c[HALF:PACK].astype(F32)).astype(BF16)
    a_y5 = ring.copy(17, "y-", put_c.at[3], got_c.at[5])

    b_z0.wait_recv()
    put_z[1, 0:RHALF] = (u[zu, 0:RHALF] + half_z[0:RHALF].astype(F32)).astype(BF16)
    put_z[1, RHALF:DP] = u[zu, RHALF:DP].astype(BF16)
    b_z2 = ring.copy(18, "zh+", put_z.at[1], got_z.at[0])
    b_z1.wait_recv()
    put_z[2, 0:RHALF] = u[zd, 0:RHALF].astype(BF16)
    put_z[2, RHALF:DP] = (u[zd, RHALF:DP] + half_z[RHALF:DP].astype(F32)).astype(BF16)
    b_z3 = ring.copy(19, "zh-", put_z.at[2], got_z.at[1])

    b_z2.wait_recv()
    b_z3.wait_recv()
    row_sum = u[zh] + got_z[0].astype(F32) + got_z[1].astype(F32)
    or_ref[...] = row_sum[:D]
    obr_ref[...] = row_sum[D : D + 1]

    loads[4].wait()
    a_z1.wait_recv()
    a_y4.wait_recv()
    a_y5.wait_recv()

    def col_sum(start, size):
        part = slice(start, start + size)
        return (
            pc[4, part].astype(F32) + got_c[3, part].astype(F32)
            + got_c[4, part].astype(F32) + got_c[5, part].astype(F32)
        )

    for t in range(FULL):
        total = col_sum(t * DP, DP)
        oc_ref[:, t * L : (t + 1) * L] = total[:D]
        obc_ref[:, t * L : (t + 1) * L] = total[D + 1 : D + 2]
    tail = col_sum(FULL * DP, QR)
    for q in range(4):
        part = pltpu.roll(tail, L - 32 * q, 1) if q else tail
        rows = min(QR, D - q * QR)
        oc_ref[q * QR : q * QR + rows, FULL * L : SHARD] = part[:rows, : SHARD - FULL * L]
        if q == 3:
            obc_ref[:, FULL * L : SHARD] = part[rows + 1 : rows + 2, : SHARD - FULL * L]
    ring.finish()


def reduce(pc, pr):
    return pl.pallas_call(
        reduce_kernel,
        out_shape=(
            jax.ShapeDtypeStruct((D, SHARD), F32),
            jax.ShapeDtypeStruct((1, SHARD), F32),
            jax.ShapeDtypeStruct((D, L), F32),
            jax.ShapeDtypeStruct((1, L), F32),
        ),
        in_specs=[ANY, ANY],
        out_specs=(IN_VMEM,) * 4,
        scratch_shapes=[
            pltpu.VMEM((5, PACK, L), BF16),
            pltpu.VMEM((4, 4, DP, L), F32),
            pltpu.VMEM((6, PACK, L), BF16),
            pltpu.VMEM((PACK, L), BF16),
            pltpu.VMEM((4, PACK, L), BF16),
            pltpu.VMEM((4, 4, DP, L), F32),
            pltpu.VMEM((2, 4, DP, L), BF16),
            pltpu.VMEM((3, 4, DP, L), BF16),
            pltpu.VMEM((2, 2, DP, L), BF16),
            pltpu.VMEM((DP, L), BF16),
            pltpu.VMEM((2, DP, L), BF16),
            pltpu.VMEM((3, DP, L), BF16),
            pltpu.VMEM((4, DP, L), F32),
            pltpu.SemaphoreType.DMA((20,)),
            pltpu.SemaphoreType.DMA((20,)),
            pltpu.SemaphoreType.DMA((6,)),
        ],
        compiler_params=pltpu.CompilerParams(
            collective_id=1, has_side_effects=True, vmem_limit_bytes=VMEM_LIMIT
        ),
        name="reduce",
    )(pc, pr)


def pad_to(a, rows, lanes):
    return jnp.pad(a, ((0, rows - a.shape[0]), (0, lanes - a.shape[1])))


def body(row_vecs, row_bias, col_vecs, col_bias, row_block, col_block, counts, block_totals):
    one_c, one_r = jnp.ones((1, SHARD), BF16), jnp.ones((1, L), BF16)
    ct = pad_to(jnp.concatenate([col_vecs.T, one_c, col_bias[None]], axis=0), 4 * QR, (FULL + 1) * L)
    rt = pad_to(jnp.concatenate([row_vecs.T, row_bias[None], one_r], axis=0), DP, L)
    gc, gr = gather(ct, rt)
    rid = row_block.reshape(CAP)
    rid = (rid % 2) * 16 + (rid // 2) % 4 * 4 + rid // 8
    cid = col_block.reshape(CAP)
    pc, pr = blocks(block_totals, rid, cid, counts.reshape(CAP, L, L), gc, gr.reshape(ROW_TILES, DP, L))
    oc, obc, orow, obr = reduce(pc, pr.reshape(2, 4, 4, DP, L))
    return orow.T, obr.reshape(L), oc.T, obc.reshape(SHARD)


def solution(mesh):
    placed = (
        P(("row", "col"), None),
        P(("row", "col")),
        P(("col", "row"), None),
        P(("col", "row")),
        P("row", "col", None),
        P("row", "col", None),
        P("row", "col", None, None, None),
        P(),
    )
    return jax.shard_map(
        body,
        mesh=mesh,
        in_specs=placed,
        out_specs=(
            P(("row", "col"), None),
            P(("row", "col")),
            P(("col", "row"), None),
            P(("col", "row")),
        ),
        check_vma=False,
    )
```

```python
import jax
import jax.numpy as jnp
from jax import lax
from jax.experimental import pallas as pl
from jax.experimental.pallas import tpu as pltpu
from jax.sharding import PartitionSpec as P

MESH = pl.DeviceIdType.MESH
ANY = pl.BlockSpec(memory_space=pl.ANY)
IN_VMEM = pl.BlockSpec(memory_space=pltpu.VMEM)
IN_SMEM = pl.BlockSpec(memory_space=pltpu.SMEM)
F32, BF16 = jnp.float32, jnp.bfloat16

D = 300
DP = 304
L = 128
SHARD = 800
FULL = SHARD // L
REST = SHARD - FULL * L
QR = 80
PACK = FULL * DP + QR
CUTS = (0, 480, 960, 1440, PACK)
RHALF = 160
SHARDS = 8
ROW_TILES = 32
COL_TILES = 50
QUAD = COL_TILES // 2
CAP = 128
GROUP = 8
VMEM_LIMIT = 56 * 1024 * 1024


def chunk(c):
    return pl.ds(CUTS[c], CUTS[c + 1] - CUTS[c])


def place():
    row, col = lax.axis_index("row"), lax.axis_index("col")
    y, zl = row % 4, row // 4
    core, x, zh = col % 2, (col // 2) % 4, col // 8
    return y, zl, core, x, zh


def row_of(y, zl):
    return zl * 4 + y


def col_of(core, x, zh):
    return (zh * 4 + x) * 2 + core


class Ring:
    def __init__(self, send, recv):
        self.send, self.recv = send, recv
        self.y, self.zl, self.core, self.x, self.zh = place()
        y, zl, core, x, zh = self.y, self.zl, self.core, self.x, self.zh
        row, col = row_of(y, zl), col_of(core, x, zh)
        self.near = {
            "y+": (row_of((y + 1) % 4, zl), col),
            "y-": (row_of((y + 3) % 4, zl), col),
            "zl": (row_of(y, 1 - zl), col),
            "x+": (row, col_of(core, (x + 1) % 4, zh)),
            "x-": (row, col_of(core, (x + 3) % 4, zh)),
            "zh+": (row, col_of(core, x, (zh + 1) % 4)),
            "zh-": (row, col_of(core, x, (zh + 3) % 4)),
            "core": (row, col_of(1 - core, x, zh)),
        }
        self.started = []

    def greet(self):
        barrier = pltpu.get_barrier_semaphore()
        for row, col in self.near.values():
            pl.semaphore_signal(barrier, inc=1, device_id={"row": row, "col": col}, device_id_type=MESH)
        return barrier

    def meet(self, barrier):
        pl.semaphore_wait(barrier, len(self.near))

    def copy(self, to, src, dst):
        row, col = self.near[to]
        k = len(self.started)
        out = pltpu.make_async_remote_copy(
            src_ref=src,
            dst_ref=dst,
            send_sem=self.send.at[k],
            recv_sem=self.recv.at[k],
            device_id={"row": row, "col": col},
            device_id_type=MESH,
        )
        out.start()
        self.started.append(out)
        return out

    def finish(self):
        for out in self.started:
            out.wait_send()


COPIES = 40


def gather_kernel(cv_ref, cb_ref, rv_ref, rb_ref, gc_ref, gr_ref, rn_ref, wc, gr, rn, last, send, recv, local):
    ring = Ring(send, recv)
    y, zl, core, x, zh = ring.y, ring.zl, ring.core, ring.x, ring.zh
    barrier = ring.greet()

    last[0:12, 0:L] = rv_ref[288:D].astype(F32)
    last[12:13, 0:L] = rb_ref[...].astype(F32)
    last[13:14, 0:L] = jnp.ones((1, L), F32)
    last[14:16, 0:L] = jnp.zeros((2, L), F32)
    gr[core, x, zh, 0:288] = rv_ref[0:288]
    gr[core, x, zh, 288:DP] = last[0:16, 0:L].astype(BF16)

    last[0:12, 0:SHARD] = cv_ref[288:D].astype(F32)
    last[12:13] = jnp.ones((1, (FULL + 1) * L), F32)
    last[13:14, 0:SHARD] = cb_ref[...].astype(F32)
    last[14:16] = jnp.zeros((2, (FULL + 1) * L), F32)
    shift = 32 * y
    lane = lax.broadcasted_iota(jnp.int32, (DP, L), 1)

    def turned(t):
        part = jnp.concatenate(
            [cv_ref[0:288, t * L : (t + 1) * L].astype(F32), last[0:16, t * L : (t + 1) * L]], axis=0
        )
        return pltpu.roll(part, shift, 1)

    before = first = turned(0)
    for t in range(1, FULL):
        part = turned(t)
        wc[t * DP : (t + 1) * DP] = jnp.where(lane < shift, before, part).astype(BF16)
        before = part
    wc[0:DP] = jnp.where(lane < shift, before, first).astype(BF16)
    part = jnp.concatenate(
        [cv_ref[0:288, FULL * L : SHARD].astype(F32), last[0:16, FULL * L : SHARD], jnp.zeros((4 * QR - DP, REST), F32)],
        axis=0,
    )
    part = jnp.concatenate([part, jnp.zeros((4 * QR, L - REST), F32)], axis=1)
    tail = part[:QR]
    for q in range(1, 4):
        tail = tail + pltpu.roll(part[q * QR : (q + 1) * QR], 32 * q, 1)
    wc[FULL * DP : PACK] = tail.astype(BF16)

    mine, other = row_of(y, zl), row_of(y, 1 - zl)
    up, down, far = row_of((y + 1) % 4, zl), row_of((y + 3) % 4, zl), row_of((y + 2) % 4, zl)
    xu, xd, xf = (x + 1) % 4, (x + 3) % 4, (x + 2) % 4
    own_c = pltpu.make_async_copy(wc, gc_ref.at[mine], local.at[0])
    own_c.start()
    outs = []

    def turn(c, xx):
        @pl.loop(0, 4)
        def _(z):
            rn[c, xx, z] = gr[c, xx, z].astype(F32).T.astype(BF16)

        for src, dst in ((gr, gr_ref), (rn, rn_ref)):
            out = pltpu.make_async_copy(src.at[c, xx], dst.at[c, xx], local.at[1 + len(outs)])
            out.start()
            outs.append(out)

    def own(to, c):
        return ring.copy(to, wc.at[chunk(c)], gc_ref.at[mine, chunk(c)])

    def pass_on(to, shard, c):
        part = gc_ref.at[shard, chunk(c)]
        return ring.copy(to, part, part)

    def rows(to, *at):
        part = gr.at[at]
        return ring.copy(to, part, part)

    ring.meet(barrier)
    r_z0 = rows("zh+", core, x, zh)
    r_z1 = rows("zh-", core, x, zh)
    c_u, c_d, c_z = {}, {}, {}
    for a, b in ((0, 2), (1, 3)):
        c_u[a], c_d[b] = own("y+", a), own("y-", b)
        c_z[a] = own("zl", a)
    c_z[2] = own("zl", 2)
    c_z[3] = own("zl", 3)

    r_z0.wait_recv()
    r_z2 = rows("zh+", core, x, (zh + 3) % 4, pl.ds(0, RHALF))
    r_z1.wait_recv()
    r_z3 = rows("zh-", core, x, (zh + 1) % 4, pl.ds(RHALF, DP - RHALF))

    f_u, f_d = {}, {}
    c_u[0].wait_recv()
    f_u[0] = pass_on("y+", down, 0)
    c_d[2].wait_recv()
    f_d[2] = pass_on("y-", up, 2)
    c_u[2], c_d[0] = own("y+", 2), own("y-", 0)

    r_z2.wait_recv()
    r_z3.wait_recv()
    r_x0 = rows("x+", core, x)
    r_x1 = rows("x-", core, x)
    r_c0 = rows("core", core, x)

    c_u[1].wait_recv()
    f_u[1] = pass_on("y+", down, 1)
    c_d[3].wait_recv()
    f_d[3] = pass_on("y-", up, 3)
    c_u[3], c_d[1] = own("y+", 3), own("y-", 1)

    turn(core, x)

    f_z = {}
    f_u[0].wait_recv()
    f_z[0] = pass_on("zl", far, 0)
    f_d[2].wait_recv()
    f_z[2] = pass_on("zl", far, 2)

    o_u, o_d = {}, {}
    c_z[0].wait_recv()
    o_u[0], o_d[0] = pass_on("y+", other, 0), pass_on("y-", other, 0)

    r_x0.wait_recv()
    r_x2 = rows("x+", core, xd, pl.ds(0, 2))
    r_c1 = rows("core", core, xd)
    r_x1.wait_recv()
    r_x3 = rows("x-", core, xu, pl.ds(2, 2))
    r_c2 = rows("core", core, xu)

    f_u[1].wait_recv()
    f_z[1] = pass_on("zl", far, 1)
    f_d[3].wait_recv()
    f_z[3] = pass_on("zl", far, 3)
    for c in (1, 2, 3):
        c_z[c].wait_recv()
        o_u[c], o_d[c] = pass_on("y+", other, c), pass_on("y-", other, c)

    turn(core, xd)
    turn(core, xu)
    r_x2.wait_recv()
    r_x3.wait_recv()
    r_c3 = rows("core", core, xf)
    turn(core, xf)
    for got, xx in ((r_c0, x), (r_c1, xd), (r_c2, xu), (r_c3, xf)):
        got.wait_recv()
        turn(1 - core, xx)

    rest = [c_u[2], c_u[3], c_d[0], c_d[1]]
    for c in range(4):
        rest += [o_u[c], o_d[c], f_z[c]]
    for got in rest:
        got.wait_recv()
    ring.finish()
    own_c.wait()
    for out in outs:
        out.wait()


def gather(cv, cb, rv, rb):
    return pl.pallas_call(
        gather_kernel,
        out_shape=(
            jax.ShapeDtypeStruct((SHARDS, PACK, L), BF16),
            jax.ShapeDtypeStruct((2, 4, 4, DP, L), BF16),
            jax.ShapeDtypeStruct((2, 4, 4, L, DP), BF16),
        ),
        in_specs=[IN_VMEM] * 4,
        out_specs=(ANY,) * 3,
        scratch_shapes=[
            pltpu.VMEM((PACK, L), BF16),
            pltpu.VMEM((2, 4, 4, DP, L), BF16),
            pltpu.VMEM((2, 4, 4, L, DP), BF16),
            pltpu.VMEM((16, (FULL + 1) * L), F32),
            pltpu.SemaphoreType.DMA((COPIES,)),
            pltpu.SemaphoreType.DMA((COPIES,)),
            pltpu.SemaphoreType.DMA((17,)),
        ],
        compiler_params=pltpu.CompilerParams(
            collective_id=0, has_side_effects=True, vmem_limit_bytes=VMEM_LIMIT
        ),
        name="gather",
    )(cv, cb, rv, rb)


def merge_tiles(ct):
    lane = lax.broadcasted_iota(jnp.int32, (DP, L), 1)

    def first(s):
        return ct[s * PACK : s * PACK + DP].astype(F32)

    def tail(s):
        part = ct[s * PACK + FULL * DP : (s + 1) * PACK].astype(F32)
        turns = [(32 * (s % 4) - 32 * q) % L for q in range(4)]
        return jnp.concatenate([pltpu.roll(part, n, 1) if n else part for n in turns], axis=0)[:DP]

    for quad in range(2):
        for k in (4, 3, 2, 1):
            s = quad * 4 + k
            tile = jnp.where(lane < 32 * k, tail(s - 1), first(s)) if k < 4 else tail(s - 1)
            if k > 1:
                tile = jnp.where(lane < 32 * (k - 1), first(s - 1), tile)
            at = s * PACK if k < 4 else SHARDS * PACK + quad * DP
            ct[at : at + DP] = tile.astype(BF16)


def tile_at(b):
    quad, j = b // QUAD, b % QUAD
    return jnp.where(j == QUAD - 1, SHARDS * PACK + quad * DP, (quad * 4 + j // FULL) * PACK + j % FULL * DP)


def pack_shard(tiles, s):
    k = s % 4
    base = (SHARD * s) // L
    lane = lax.broadcasted_iota(jnp.int32, (DP, L), 1)
    lane_q = lax.broadcasted_iota(jnp.int32, (QR, L), 1)
    after = tiles[base + FULL]
    head = tiles[base]
    if k:
        head = jnp.where(lane < 32 * k, after, head)
    parts = [(0, head)] + [(t * DP, tiles[base + t]) for t in range(1, FULL)]
    after = jnp.concatenate([after, jnp.zeros((4 * QR - DP, L), F32)], axis=0)
    tail = None
    for q in range(4):
        n = (32 * q - 32 * k) % L
        part = after[q * QR : (q + 1) * QR]
        part = pltpu.roll(part, n, 1) if n else part
        tail = part if q == 0 else jnp.where(lane_q < 32 * q, tail, part)
    return parts + [(FULL * DP, tail)]


LOG2_100 = 6.643856189774724
LN2 = 0.6931471805599453


def blocks_kernel(total_ref, rid_ref, cid_ref, counts_ref, gc_ref, gr_ref, rn_ref, pc_ref, pr_ref,
                  counts, ct, rt, rn, acc_c, acc_r, sems, count_sems):
    row, col = lax.axis_index("row"), lax.axis_index("col")
    total = total_ref[row, col]
    groups = (total + GROUP - 1) // GROUP
    loads = [
        pltpu.make_async_copy(gc_ref.at[s], ct.at[pl.ds(s * PACK, PACK)], sems.at[s]) for s in range(SHARDS)
    ]
    loads.append(pltpu.make_async_copy(rn_ref, rn, sems.at[8]))
    loads.append(pltpu.make_async_copy(gr_ref, rt, sems.at[9]))
    for one in loads:
        one.start()

    def load(g):
        part = pl.ds(g * GROUP, GROUP)
        return pltpu.make_async_copy(counts_ref.at[part], counts.at[part], count_sems.at[g])

    @pl.loop(0, groups)
    def _(g):
        load(g).start()

    @pl.loop(0, COL_TILES)
    def _(i):
        acc_c[i] = jnp.zeros((DP, L), F32)

    @pl.loop(0, ROW_TILES)
    def _(i):
        acc_r[i] = jnp.zeros((DP, L), F32)

    for one in loads[:8]:
        one.wait()
    merge_tiles(ct)
    for one in loads[8:]:
        one.wait()

    @pl.loop(0, groups)
    def _(g):
        load(g).wait()
        terms, rids, cids, tiles = [], [], [], []
        for k in range(GROUP):
            n = g * GROUP + k
            rid, cid = rid_ref[0, 0, n], cid_ref[0, 0, n]
            rid = rid % 2 * 16 + rid // 2 % 4 * 4 + rid // 8
            rids.append(rid)
            cids.append(cid)
            tile = pl.ds(pl.multiple_of(tile_at(cid), 16), DP)
            tiles.append(tile)
            scores = jnp.dot(rn[rid], ct[tile], preferred_element_type=F32)
            x = counts[n]
            least = jnp.where(n < total, 0, jnp.int32(2**31 - 1))
            log2x = jnp.log2(jnp.maximum(x.astype(F32), 1.0))
            weight2 = jnp.exp2(jnp.minimum(0.75 * log2x + (1.0 - 0.75 * LOG2_100), 1.0))
            term = weight2 * (scores - LN2 * log2x)
            terms.append(jnp.where(x > least, term, 0.0).astype(BF16))
        for k in range(GROUP):
            acc_c[cids[k]] += jnp.dot(rt[rids[k]], terms[k], preferred_element_type=F32)
            acc_r[rids[k]] += lax.dot_general(
                ct[tiles[k]], terms[k], (((1,), (1,)), ((), ())), preferred_element_type=F32
            )

    outs = [pltpu.make_async_copy(acc_r, pr_ref, sems.at[8])]
    outs[0].start()
    for s in range(SHARDS):
        for at, part in pack_shard(acc_c, s):
            ct[s * PACK + at : s * PACK + at + part.shape[0]] = part.astype(BF16)
        outs.append(pltpu.make_async_copy(ct.at[pl.ds(s * PACK, PACK)], pc_ref.at[s], sems.at[s]))
        outs[-1].start()
    for out in outs:
        out.wait()


def blocks(totals, rid, cid, counts, gc, gr, rn):
    return pl.pallas_call(
        blocks_kernel,
        out_shape=(
            jax.ShapeDtypeStruct((SHARDS, PACK, L), BF16),
            jax.ShapeDtypeStruct((ROW_TILES, DP, L), F32),
        ),
        in_specs=[IN_SMEM] * 3 + [ANY] * 4,
        out_specs=(ANY, ANY),
        scratch_shapes=[
            pltpu.VMEM((CAP, L, L), jnp.int32),
            pltpu.VMEM((SHARDS * PACK + 2 * DP, L), BF16),
            pltpu.VMEM((ROW_TILES, DP, L), BF16),
            pltpu.VMEM((ROW_TILES, L, DP), BF16),
            pltpu.VMEM((COL_TILES, DP, L), F32),
            pltpu.VMEM((ROW_TILES, DP, L), F32),
            pltpu.SemaphoreType.DMA((10,)),
            pltpu.SemaphoreType.DMA((CAP // GROUP,)),
        ],
        compiler_params=pltpu.CompilerParams(vmem_limit_bytes=VMEM_LIMIT),
        name="blocks",
    )(totals, rid, cid, counts, gc, gr, rn)


def reduce_kernel(pc_ref, pr_ref, oc_ref, or_ref,
                  pc, pr, got_c, half_c, put_c, got_core, got_x, put_x, half_x, half_z, got_z, put_z, u,
                  send, recv, local):
    ring = Ring(send, recv)
    y, zl, core, x, zh = ring.y, ring.zl, ring.core, ring.x, ring.zh
    zo = 1 - zl
    barrier = ring.greet()
    up, down, far = (y + 1) % 4, (y + 3) % 4, (y + 2) % 4
    xu, xd, xf = (x + 1) % 4, (x + 3) % 4, (x + 2) % 4
    zu, zd, zf = (zh + 1) % 4, (zh + 3) % 4, (zh + 2) % 4
    FAR, OTHER, UP, DOWN, MINE = range(5)
    wanted = (row_of(far, zl), row_of(y, zo), row_of(up, zl), row_of(down, zl), row_of(y, zl))
    loads = [pltpu.make_async_copy(pc_ref.at[w], pc.at[i], local.at[i]) for i, w in enumerate(wanted)]
    load_r = pltpu.make_async_copy(pr_ref.at[core], pr, local.at[5])
    loads[FAR].start()
    load_r.start()
    for k in range(1, 5):
        loads[k].start()
    ring.meet(barrier)

    def raw(to, y_to, c, k):
        return ring.copy(to, pc_ref.at[row_of(y_to, zo), chunk(c)], got_c.at[k, chunk(c)])

    def put(to, k, c, dst):
        return ring.copy(to, put_c.at[k, chunk(c)], dst.at[chunk(c)])

    def total(k, c, *more):
        at = chunk(c)
        out = pc[k, at].astype(F32)
        for one in more:
            out = out + one[at].astype(F32)
        return out

    a_z, a_u, a_d = {}, {}, {}
    for c in (0, 1):
        a_z[2 * c] = raw("zl", far, 2 * c, 0)
        a_u[c], a_d[c] = raw("y+", up, c, 1), raw("y-", down, c, 2)
    for c in (1, 3):
        a_z[c] = raw("zl", far, c, 0)
    b_c = [ring.copy("core", pr_ref.at[1 - core, w], got_core.at[k]) for k, w in enumerate((xf, xu, xd, x))]
    for one in loads:
        one.wait()
    load_r.wait()

    q2 = {}

    def pass_far(c):
        a_z[c].wait_recv()
        put_c[0, chunk(c)] = total(FAR, c, got_c.at[0]).astype(BF16)
        q2[c] = put("y+" if c < 2 else "y-", 0, c, half_c)

    qz = {}

    def pass_other(c):
        a_u[c].wait_recv()
        a_d[c].wait_recv()
        put_c[1, chunk(c)] = total(OTHER, c, got_c.at[1], got_c.at[2]).astype(BF16)
        qz[c] = put("zl", 1, c, got_c.at[3])

    q_u, q_d = {}, {}

    def pass_near(c):
        q2[c].wait_recv()
        if c < 2:
            put_c[2, chunk(c)] = total(UP, c, half_c).astype(BF16)
            q_u[c] = put("y+", 2, c, got_c.at[4])
        else:
            put_c[2, chunk(c)] = total(DOWN, c, half_c).astype(BF16)
            q_d[c] = put("y-", 2, c, got_c.at[5])

    def pass_plain(c):
        if c < 2:
            q_d[c] = ring.copy("y-", pc.at[DOWN, chunk(c)], got_c.at[5, chunk(c)])
        else:
            q_u[c] = ring.copy("y+", pc.at[UP, chunk(c)], got_c.at[4, chunk(c)])

    pass_far(0)
    a_u[2], a_d[2] = raw("y+", up, 2, 1), raw("y-", down, 2, 2)
    b_c[0].wait_recv()
    for z in range(4):
        put_x[0, z] = (pr[xf, z] + got_core[0, z]).astype(BF16)
    b_x0 = ring.copy("x+", put_x.at[0, pl.ds(0, 2)], half_x.at[0])
    b_x1 = ring.copy("x-", put_x.at[0, pl.ds(2, 2)], half_x.at[1])
    pass_far(2)
    a_u[3], a_d[3] = raw("y+", up, 3, 1), raw("y-", down, 3, 2)
    pass_other(0)
    pass_far(1)
    pass_other(1)

    b_c[1].wait_recv()
    b_x0.wait_recv()
    for z in range(4):
        one = pr[xu, z] + got_core[1, z]
        if z < 2:
            one = one + half_x[0, z].astype(F32)
        put_x[1, z] = one.astype(BF16)
    b_x2 = ring.copy("x+", put_x.at[1], got_x.at[0])
    b_c[2].wait_recv()
    b_x1.wait_recv()
    for z in range(4):
        one = pr[xd, z] + got_core[2, z]
        if z >= 2:
            one = one + half_x[1, z - 2].astype(F32)
        put_x[2, z] = one.astype(BF16)
    b_x3 = ring.copy("x-", put_x.at[2], got_x.at[1])

    pass_far(3)
    pass_plain(0)
    pass_plain(2)
    pass_near(0)
    pass_near(2)
    pass_other(2)
    pass_plain(1)
    pass_plain(3)
    pass_near(1)
    pass_near(3)
    pass_other(3)

    b_c[3].wait_recv()
    b_x2.wait_recv()
    b_x3.wait_recv()
    for z in range(4):
        u[z] = pr[x, z] + got_core[3, z] + got_x[0, z].astype(F32) + got_x[1, z].astype(F32)
    put_z[0] = u[zf].astype(BF16)
    rlo, rhi = pl.ds(0, RHALF), pl.ds(RHALF, DP - RHALF)
    b_z0 = ring.copy("zh+", put_z.at[0, rlo], half_z.at[rlo])
    b_z1 = ring.copy("zh-", put_z.at[0, rhi], half_z.at[rhi])
    b_z0.wait_recv()
    put_z[1, 0:RHALF] = (u[zu, 0:RHALF] + half_z[0:RHALF].astype(F32)).astype(BF16)
    put_z[1, RHALF:DP] = u[zu, RHALF:DP].astype(BF16)
    b_z2 = ring.copy("zh+", put_z.at[1], got_z.at[0])
    b_z1.wait_recv()
    put_z[2, 0:RHALF] = u[zd, 0:RHALF].astype(BF16)
    put_z[2, RHALF:DP] = (u[zd, RHALF:DP] + half_z[RHALF:DP].astype(F32)).astype(BF16)
    b_z3 = ring.copy("zh-", put_z.at[2], got_z.at[1])

    for c in range(4):
        for got in (qz, q_u, q_d):
            got[c].wait_recv()

    def col_sum(start, size):
        at = pl.ds(start, size)
        return (
            pc[MINE, at].astype(F32) + got_c[3, at].astype(F32)
            + got_c[4, at].astype(F32) + got_c[5, at].astype(F32)
        )

    shift = 32 * y
    back = (L - shift) % L
    lane = lax.broadcasted_iota(jnp.int32, (DP, L), 1)
    sums = [col_sum(t * DP, DP) for t in range(FULL)]
    for t in range(FULL):
        oc_ref[:, t * L : (t + 1) * L] = pltpu.roll(
            jnp.where(lane < shift, sums[(t + 1) % FULL], sums[t]), back, 1
        )
    tail = col_sum(FULL * DP, QR)
    for q in range(4):
        part = pltpu.roll(tail, L - 32 * q, 1) if q else tail
        rows = min(QR, DP - q * QR)
        oc_ref[q * QR : q * QR + rows, FULL * L :] = part[:rows]

    b_z2.wait_recv()
    b_z3.wait_recv()
    or_ref[...] = u[zh] + got_z[0].astype(F32) + got_z[1].astype(F32)
    ring.finish()


def reduce(pc, pr):
    return pl.pallas_call(
        reduce_kernel,
        out_shape=(
            jax.ShapeDtypeStruct((DP, (FULL + 1) * L), F32),
            jax.ShapeDtypeStruct((DP, L), F32),
        ),
        in_specs=[ANY, ANY],
        out_specs=(IN_VMEM,) * 2,
        scratch_shapes=[
            pltpu.VMEM((5, PACK, L), BF16),
            pltpu.VMEM((4, 4, DP, L), F32),
            pltpu.VMEM((6, PACK, L), BF16),
            pltpu.VMEM((PACK, L), BF16),
            pltpu.VMEM((3, PACK, L), BF16),
            pltpu.VMEM((4, 4, DP, L), F32),
            pltpu.VMEM((2, 4, DP, L), BF16),
            pltpu.VMEM((3, 4, DP, L), BF16),
            pltpu.VMEM((2, 2, DP, L), BF16),
            pltpu.VMEM((DP, L), BF16),
            pltpu.VMEM((2, DP, L), BF16),
            pltpu.VMEM((3, DP, L), BF16),
            pltpu.VMEM((4, DP, L), F32),
            pltpu.SemaphoreType.DMA((COPIES,)),
            pltpu.SemaphoreType.DMA((COPIES,)),
            pltpu.SemaphoreType.DMA((6,)),
        ],
        compiler_params=pltpu.CompilerParams(
            collective_id=1, has_side_effects=True, vmem_limit_bytes=VMEM_LIMIT
        ),
        name="reduce",
    )(pc, pr)


def outputs_kernel(oc_ref, or_ref, row_ref, row_bias_ref, col_ref, col_bias_ref):
    col_ref[...] = oc_ref[:D, :SHARD]
    col_bias_ref[...] = oc_ref[D + 1, :SHARD]
    row_ref[...] = or_ref[:D]
    row_bias_ref[...] = or_ref[D]


def outputs(oc, orow):
    return pl.pallas_call(
        outputs_kernel,
        out_shape=(
            jax.ShapeDtypeStruct((D, L), F32),
            jax.ShapeDtypeStruct((L,), F32),
            jax.ShapeDtypeStruct((D, SHARD), F32),
            jax.ShapeDtypeStruct((SHARD,), F32),
        ),
        in_specs=[IN_VMEM] * 2,
        out_specs=(IN_VMEM,) * 4,
        name="outputs",
    )(oc, orow)


def body(row_vecs, row_bias, col_vecs, col_bias, row_block, col_block, counts, block_totals):
    gc, gr, rn = gather(col_vecs.T, col_bias[None], row_vecs.T, row_bias[None])
    pc, pr = blocks(
        block_totals, row_block, col_block, counts.reshape(CAP, L, L), gc,
        gr.reshape(ROW_TILES, DP, L), rn.reshape(ROW_TILES, L, DP),
    )
    grad_rows, grad_row_bias, grad_cols, grad_col_bias = outputs(*reduce(pc, pr.reshape(2, 4, 4, DP, L)))
    return grad_rows.T, grad_row_bias, grad_cols.T, grad_col_bias


def solution(mesh):
    placed = (
        P(("row", "col"), None),
        P(("row", "col")),
        P(("col", "row"), None),
        P(("col", "row")),
        P("row", "col", None),
        P("row", "col", None),
        P("row", "col", None, None, None),
        P(),
    )
    return jax.shard_map(
        body,
        mesh=mesh,
        in_specs=placed,
        out_specs=(
            P(("row", "col"), None),
            P(("row", "col")),
            P(("col", "row"), None),
            P(("col", "row")),
        ),
        check_vma=False,
    )
```

```python
import jax
import jax.numpy as jnp
from jax import lax
from jax.experimental import pallas as pl
from jax.experimental.pallas import tpu as pltpu
from jax.sharding import PartitionSpec as P

MESH = pl.DeviceIdType.MESH
IN_HBM = pl.BlockSpec(memory_space=pltpu.HBM)
IN_VMEM = pl.BlockSpec(memory_space=pltpu.VMEM)
IN_SMEM = pl.BlockSpec(memory_space=pltpu.SMEM)
F32, BF16 = jnp.float32, jnp.bfloat16

D = 300
DP = 304
L = 128
SHARD = 800
FULL = SHARD // L
REST = SHARD - FULL * L
QR = 80
PACK = FULL * DP + QR
CUTS = (0, 480, 960, 1440, PACK)
RHALF = 160
SHARDS = 8
ROW_TILES = 32
COL_TILES = 50
QUAD = COL_TILES // 2
CAP = 128
TILES = SHARDS * PACK + 8 * DP
GROUP = 16
MIB = 1024 * 1024


def chunk(c):
    return pl.ds(CUTS[c], CUTS[c + 1] - CUTS[c])


def place():
    row, col = lax.axis_index("row"), lax.axis_index("col")
    y, zl = row % 4, row // 4
    core, x, zh = col % 2, (col // 2) % 4, col // 8
    return y, zl, core, x, zh


def row_of(y, zl):
    return zl * 4 + y


def col_of(core, x, zh):
    return (zh * 4 + x) * 2 + core


class Ring:
    def __init__(self, send, recv):
        self.send, self.recv = send, recv
        self.y, self.zl, self.core, self.x, self.zh = place()
        y, zl, core, x, zh = self.y, self.zl, self.core, self.x, self.zh
        row, col = row_of(y, zl), col_of(core, x, zh)
        self.near = {
            "y+": (row_of((y + 1) % 4, zl), col),
            "y-": (row_of((y + 3) % 4, zl), col),
            "zl": (row_of(y, 1 - zl), col),
            "x+": (row, col_of(core, (x + 1) % 4, zh)),
            "x-": (row, col_of(core, (x + 3) % 4, zh)),
            "zh+": (row, col_of(core, x, (zh + 1) % 4)),
            "zh-": (row, col_of(core, x, (zh + 3) % 4)),
            "core": (row, col_of(1 - core, x, zh)),
        }
        self.started = []

    def greet(self):
        barrier = pltpu.get_barrier_semaphore()
        for row, col in self.near.values():
            pl.semaphore_signal(barrier, inc=1, device_id={"row": row, "col": col}, device_id_type=MESH)
        return barrier

    def meet(self, barrier):
        pl.semaphore_wait(barrier, len(self.near))

    def copy(self, to, src, dst):
        row, col = self.near[to]
        k = len(self.started)
        out = pltpu.make_async_remote_copy(
            src_ref=src,
            dst_ref=dst,
            send_sem=self.send.at[k],
            recv_sem=self.recv.at[k],
            device_id={"row": row, "col": col},
            device_id_type=MESH,
        )
        out.start()
        self.started.append(out)
        return out

    def finish(self):
        for out in self.started:
            out.wait_send()


COPIES = 48


def gather_kernel(cv_hbm, cb_hbm, rv_hbm, rb_hbm, counts_hbm, gc, gr, rn, counts,
                  cv_ref, cb_ref, rv_ref, rb_ref, wc, last, send, recv, local):
    pairs = ((rv_hbm, rv_ref), (rb_hbm, rb_ref), (cv_hbm, cv_ref), (cb_hbm, cb_ref), (counts_hbm, counts))
    loads = [pltpu.make_async_copy(src, dst, local.at[1 + k]) for k, (src, dst) in enumerate(pairs)]
    for load in loads:
        load.start()
    ring = Ring(send, recv)
    y, zl, core, x, zh = ring.y, ring.zl, ring.core, ring.x, ring.zh
    barrier = ring.greet()

    for load in loads[:2]:
        load.wait()
    last[0:12, 0:L] = rv_ref[288:D].astype(F32)
    last[12:13, 0:L] = rb_ref[...].astype(F32).reshape(1, L)
    last[13:14, 0:L] = jnp.ones((1, L), F32)
    last[14:16, 0:L] = jnp.zeros((2, L), F32)
    gr[core, x, zh, 0:288] = rv_ref[0:288]
    gr[core, x, zh, 288:DP] = last[0:16, 0:L].astype(BF16)

    for load in loads[2:4]:
        load.wait()
    last[0:12, 0:SHARD] = cv_ref[288:D].astype(F32)
    last[12:13] = jnp.ones((1, (FULL + 1) * L), F32)
    last[13:14, 0:SHARD] = cb_ref[...].astype(F32).reshape(1, SHARD)
    last[14:16] = jnp.zeros((2, (FULL + 1) * L), F32)
    shift = 32 * y
    lane = lax.broadcasted_iota(jnp.int32, (DP, L), 1)

    def turned(t):
        part = jnp.concatenate(
            [cv_ref[0:288, t * L : (t + 1) * L].astype(F32), last[0:16, t * L : (t + 1) * L]], axis=0
        )
        return pltpu.roll(part, shift, 1)

    before = first = turned(0)
    for t in range(1, FULL):
        part = turned(t)
        wc[t * DP : (t + 1) * DP] = jnp.where(lane < shift, before, part).astype(BF16)
        before = part
    wc[0:DP] = jnp.where(lane < shift, before, first).astype(BF16)
    part = jnp.concatenate(
        [cv_ref[0:288, FULL * L : SHARD].astype(F32), last[0:16, FULL * L : SHARD], jnp.zeros((4 * QR - DP, REST), F32)],
        axis=0,
    )
    part = jnp.concatenate([part, jnp.zeros((4 * QR, L - REST), F32)], axis=1)
    tail = part[:QR]
    for q in range(1, 4):
        tail = tail + pltpu.roll(part[q * QR : (q + 1) * QR], 32 * q, 1)
    wc[FULL * DP : PACK] = tail.astype(BF16)

    mine, other = row_of(y, zl), row_of(y, 1 - zl)
    up, down, far = row_of((y + 1) % 4, zl), row_of((y + 3) % 4, zl), row_of((y + 2) % 4, zl)
    xu, xd, xf = (x + 1) % 4, (x + 3) % 4, (x + 2) % 4
    own_c = pltpu.make_async_copy(wc, gc.at[pl.ds(mine * PACK, PACK)], local.at[0])
    own_c.start()

    def turn(c, xx):
        @pl.loop(0, 4)
        def _(z):
            rn[c, xx, z] = gr[c, xx, z].astype(F32).T.astype(BF16)

    def part_of(shard, c):
        return gc.at[pl.ds(pl.multiple_of(shard * PACK + CUTS[c], 16), CUTS[c + 1] - CUTS[c])]

    def own(to, c):
        return ring.copy(to, wc.at[chunk(c)], part_of(mine, c))

    def pass_on(to, shard, c):
        return ring.copy(to, part_of(shard, c), part_of(shard, c))

    def rows(to, *at):
        return ring.copy(to, gr.at[at], gr.at[at])

    zu, zd, zf = (zh + 1) % 4, (zh + 3) % 4, (zh + 2) % 4
    ring.meet(barrier)
    r_zu = rows("zh+", core, x, zh)
    r_zd = rows("zh-", core, x, zh)
    x_u, x_d, x_f = {}, {}, {}
    x_u["own"], x_d["own"] = rows("x+", core, x, zh), rows("x-", core, x, zh)
    c_u, c_d, c_z = {}, {}, {}
    for a, b in ((0, 2), (1, 3)):
        c_u[a], c_d[b] = own("y+", a), own("y-", b)
        c_z[a] = own("zl", a)

    f_u, f_d, f_z, o_u, o_d = {}, {}, {}, {}, {}
    c_u[0].wait_recv()
    f_u[0] = pass_on("y+", down, 0)
    c_d[2].wait_recv()
    f_d[2] = pass_on("y-", up, 2)
    c_u[2], c_d[0] = own("y+", 2), own("y-", 0)
    c_z[2] = own("zl", 2)

    r_zu.wait_recv()
    r_fu = rows("zh+", core, x, zd, pl.ds(0, RHALF))
    x_u["zd"], x_d["zd"] = rows("x+", core, x, zd), rows("x-", core, x, zd)
    r_zd.wait_recv()
    r_fd = rows("zh-", core, x, zu, pl.ds(RHALF, DP - RHALF))
    x_u["zu"], x_d["zu"] = rows("x+", core, x, zu), rows("x-", core, x, zu)

    c_u[1].wait_recv()
    f_u[1] = pass_on("y+", down, 1)
    c_d[3].wait_recv()
    f_d[3] = pass_on("y-", up, 3)
    c_u[3], c_d[1] = own("y+", 3), own("y-", 1)
    c_z[3] = own("zl", 3)

    x_u["own"].wait_recv()
    x_f["own"] = rows("x+", core, xd, zh)

    f_u[0].wait_recv()
    f_z[0] = pass_on("zl", far, 0)
    f_d[2].wait_recv()
    f_z[2] = pass_on("zl", far, 2)

    r_fu.wait_recv()
    r_fd.wait_recv()
    x_u["zf"], x_d["zf"] = rows("x+", core, x, zf), rows("x-", core, x, zf)
    x_d["zd"].wait_recv()
    x_f["zd"] = rows("x-", core, xu, zd)
    x_u["zu"].wait_recv()
    x_f["zu"] = rows("x+", core, xd, zu)
    c_z[0].wait_recv()
    o_u[0], o_d[0] = pass_on("y+", other, 0), pass_on("y-", other, 0)

    f_u[1].wait_recv()
    f_z[1] = pass_on("zl", far, 1)
    f_d[3].wait_recv()
    f_z[3] = pass_on("zl", far, 3)
    k_own = rows("core", core, x)
    for c in (1, 2):
        c_z[c].wait_recv()
        o_u[c], o_d[c] = pass_on("y+", other, c), pass_on("y-", other, c)

    x_d["zf"].wait_recv()
    x_f["zf"] = rows("x-", core, xu, zf)
    for one in (x_d["own"], x_d["zu"]):
        one.wait_recv()
    k_up = rows("core", core, xu)
    for one in (x_u["zd"], x_u["zf"]):
        one.wait_recv()
    k_down = rows("core", core, xd)
    c_z[3].wait_recv()
    o_u[3], o_d[3] = pass_on("y+", other, 3), pass_on("y-", other, 3)

    turn(core, x)
    for one in x_f.values():
        one.wait_recv()
    k_far = rows("core", core, xf)
    for xx in (xd, xu, xf):
        turn(core, xx)
    for got, xx in ((k_own, x), (k_up, xu), (k_down, xd), (k_far, xf)):
        got.wait_recv()
        turn(1 - core, xx)

    rest = [c_u[2], c_u[3], c_d[0], c_d[1]]
    for c in range(4):
        rest += [o_u[c], o_d[c], f_z[c]]
    for got in rest:
        got.wait_recv()
    own_c.wait()
    merge_tiles(gc)
    ring.finish()
    loads[4].wait()


def gather(cv, cb, rv, rb, counts):
    return pl.pallas_call(
        gather_kernel,
        out_shape=(
            pltpu.VMEM((TILES, L), BF16),
            pltpu.VMEM((2, 4, 4, DP, L), BF16),
            pltpu.VMEM((2, 4, 4, L, DP), BF16),
            pltpu.VMEM((CAP, L, L), jnp.int32),
        ),
        in_specs=[IN_HBM] * 5,
        out_specs=(IN_VMEM,) * 4,
        scratch_shapes=[
            pltpu.VMEM((D, SHARD), BF16),
            pltpu.VMEM((SHARD,), BF16),
            pltpu.VMEM((D, L), BF16),
            pltpu.VMEM((L,), BF16),
            pltpu.VMEM((PACK, L), BF16),
            pltpu.VMEM((16, (FULL + 1) * L), F32),
            pltpu.SemaphoreType.DMA((COPIES,)),
            pltpu.SemaphoreType.DMA((COPIES,)),
            pltpu.SemaphoreType.DMA((6,)),
        ],
        compiler_params=pltpu.CompilerParams(
            collective_id=0, has_side_effects=True, vmem_limit_bytes=8 * MIB
        ),
        name="gather",
    )(*(pltpu.with_memory_space_constraint(a, pltpu.HBM) for a in (cv, cb, rv, rb, counts)))


def merge_tiles(ct):
    lane = lax.broadcasted_iota(jnp.int32, (DP, L), 1)

    def first(s):
        return ct[s * PACK : s * PACK + DP].astype(F32)

    def tail(s):
        part = ct[s * PACK + FULL * DP : (s + 1) * PACK].astype(F32)
        turns = [(32 * (s % 4) - 32 * q) % L for q in range(4)]
        return jnp.concatenate([pltpu.roll(part, n, 1) if n else part for n in turns], axis=0)[:DP]

    for s in range(SHARDS):
        k = s % 4
        tile = tail(s)
        if k:
            tile = jnp.where(lane < 32 * k, first(s), tile)
        if k < 3:
            tile = jnp.where(lane < 32 * (k + 1), tile, first(s + 1))
        at = SHARDS * PACK + s * DP
        ct[at : at + DP] = tile.astype(BF16)


def tile_at(b):
    quad, j = b // QUAD, b % QUAD
    k, t = j // FULL, j % FULL
    shared = (k > 0) & (t == 0)
    return jnp.where(shared, SHARDS * PACK + (quad * 4 + k - 1) * DP, (quad * 4 + k) * PACK + t * DP)


def pack_shard(tiles, s):
    k = s % 4
    base = (SHARD * s) // L
    lane = lax.broadcasted_iota(jnp.int32, (DP, L), 1)
    lane_q = lax.broadcasted_iota(jnp.int32, (QR, L), 1)
    after = tiles[base + FULL]
    head = tiles[base]
    if k:
        head = jnp.where(lane < 32 * k, after, head)
    parts = [(0, head)] + [(t * DP, tiles[base + t]) for t in range(1, FULL)]
    after = jnp.concatenate([after, jnp.zeros((4 * QR - DP, L), F32)], axis=0)
    tail = None
    for q in range(4):
        n = (32 * q - 32 * k) % L
        part = after[q * QR : (q + 1) * QR]
        part = pltpu.roll(part, n, 1) if n else part
        tail = part if q == 0 else jnp.where(lane_q < 32 * q, tail, part)
    return parts + [(FULL * DP, tail)]


LOG2_100 = 6.643856189774724
LN2 = 0.6931471805599453


def blocks_kernel(total_ref, rid_ref, cid_ref, counts, ct, rt, rn, pc, acc_r, acc_c):
    row, col = lax.axis_index("row"), lax.axis_index("col")
    total = total_ref[row, col]
    groups = (total + GROUP - 1) // GROUP

    @pl.loop(0, COL_TILES)
    def _(i):
        acc_c[i] = jnp.zeros((DP, L), F32)

    @pl.loop(0, ROW_TILES)
    def _(i):
        acc_r[i] = jnp.zeros((DP, L), F32)

    @pl.loop(0, groups)
    def _(g):
        terms, rids, cids, tiles = [], [], [], []
        for k in range(GROUP):
            n = g * GROUP + k
            rid, cid = rid_ref[0, 0, n], cid_ref[0, 0, n]
            rid = rid % 2 * 16 + rid // 2 % 4 * 4 + rid // 8
            rids.append(rid)
            cids.append(cid)
            tile = pl.ds(pl.multiple_of(tile_at(cid), 16), DP)
            tiles.append(tile)
            scores = jnp.dot(rn[rid], ct[tile], preferred_element_type=F32)
            x = counts[n]
            least = jnp.where(n < total, 0, jnp.int32(2**31 - 1))
            log2x = jnp.log2(jnp.maximum(x.astype(F32), 1.0))
            weight2 = jnp.exp2(jnp.minimum(0.75 * log2x + (1.0 - 0.75 * LOG2_100), 1.0))
            term = weight2 * (scores - LN2 * log2x)
            terms.append(jnp.where(x > least, term, 0.0).astype(BF16))
        for k in range(GROUP):
            term, none = terms[k], jnp.zeros((L, L), BF16)
            both = jnp.concatenate(
                [jnp.concatenate([term, none], axis=1), jnp.concatenate([none, term.T], axis=1)], axis=0
            )
            vecs = jnp.concatenate([rt[rids[k]], ct[tiles[k]]], axis=1)
            grads = jnp.dot(vecs, both, preferred_element_type=F32)
            acc_c[cids[k]] += grads[:, :L]
            acc_r[rids[k]] += grads[:, L:]

    for s in range(SHARDS):
        for at, part in pack_shard(acc_c, s):
            pc[s, at : at + part.shape[0]] = part.astype(BF16)


def blocks(totals, rid, cid, counts, gc, gr, rn):
    return pl.pallas_call(
        blocks_kernel,
        out_shape=(
            pltpu.VMEM((SHARDS, PACK, L), BF16),
            pltpu.VMEM((ROW_TILES, DP, L), F32),
        ),
        in_specs=[IN_SMEM] * 3 + [IN_VMEM] * 4,
        out_specs=(IN_VMEM, IN_VMEM),
        scratch_shapes=[pltpu.VMEM((COL_TILES, DP, L), F32)],
        compiler_params=pltpu.CompilerParams(vmem_limit_bytes=14 * MIB),
        name="blocks",
    )(totals, rid, cid, counts, gc, gr, rn)


def reduce_kernel(pc_ref, pr_ref, oc_ref, or_ref,
                  got_c, half_c, put_c, got_core, got_x, put_x, half_x, half_z, got_z, put_z, u,
                  send, recv):
    ring = Ring(send, recv)
    y, zl, core, x, zh = ring.y, ring.zl, ring.core, ring.x, ring.zh
    zo = 1 - zl
    barrier = ring.greet()
    up, down, far = (y + 1) % 4, (y + 3) % 4, (y + 2) % 4
    xu, xd, xf = (x + 1) % 4, (x + 3) % 4, (x + 2) % 4
    zu, zd, zf = (zh + 1) % 4, (zh + 3) % 4, (zh + 2) % 4
    FAR, OTHER, UP, DOWN, MINE = range(5)
    wanted = (row_of(far, zl), row_of(y, zo), row_of(up, zl), row_of(down, zl), row_of(y, zl))
    pr = pr_ref.at[core]
    ring.meet(barrier)

    def raw(to, y_to, c, k):
        return ring.copy(to, pc_ref.at[row_of(y_to, zo), chunk(c)], got_c.at[k, chunk(c)])

    def put(to, k, c, dst):
        return ring.copy(to, put_c.at[k, chunk(c)], dst.at[chunk(c)])

    def total(k, c, *more):
        at = chunk(c)
        out = pc_ref[wanted[k], at].astype(F32)
        for one in more:
            out = out + one[at].astype(F32)
        return out

    a_z, a_u, a_d = {}, {}, {}
    for c in (0, 1):
        a_z[2 * c] = raw("zl", far, 2 * c, 0)
        a_u[c], a_d[c] = raw("y+", up, c, 1), raw("y-", down, c, 2)
    for c in (1, 3):
        a_z[c] = raw("zl", far, c, 0)
    b_c = [ring.copy("core", pr_ref.at[1 - core, w], got_core.at[k]) for k, w in enumerate((xf, xu, xd, x))]

    q2 = {}

    def pass_far(c):
        a_z[c].wait_recv()
        put_c[0, chunk(c)] = total(FAR, c, got_c.at[0]).astype(BF16)
        q2[c] = put("y+" if c < 2 else "y-", 0, c, half_c)

    qz = {}

    def pass_other(c):
        a_u[c].wait_recv()
        a_d[c].wait_recv()
        put_c[1, chunk(c)] = total(OTHER, c, got_c.at[1], got_c.at[2]).astype(BF16)
        qz[c] = put("zl", 1, c, got_c.at[3])

    q_u, q_d = {}, {}

    def pass_near(c):
        q2[c].wait_recv()
        if c < 2:
            put_c[2, chunk(c)] = total(UP, c, half_c).astype(BF16)
            q_u[c] = put("y+", 2, c, got_c.at[4])
        else:
            put_c[2, chunk(c)] = total(DOWN, c, half_c).astype(BF16)
            q_d[c] = put("y-", 2, c, got_c.at[5])

    def pass_plain(c):
        if c < 2:
            q_d[c] = ring.copy("y-", pc_ref.at[wanted[DOWN], chunk(c)], got_c.at[5, chunk(c)])
        else:
            q_u[c] = ring.copy("y+", pc_ref.at[wanted[UP], chunk(c)], got_c.at[4, chunk(c)])

    pass_far(0)
    a_u[2], a_d[2] = raw("y+", up, 2, 1), raw("y-", down, 2, 2)
    b_c[0].wait_recv()
    for z in range(4):
        put_x[0, z] = (pr[xf, z] + got_core[0, z]).astype(BF16)
    b_x0 = ring.copy("x+", put_x.at[0, pl.ds(0, 2)], half_x.at[0])
    b_x1 = ring.copy("x-", put_x.at[0, pl.ds(2, 2)], half_x.at[1])
    pass_far(2)
    a_u[3], a_d[3] = raw("y+", up, 3, 1), raw("y-", down, 3, 2)
    pass_other(0)
    pass_far(1)
    pass_other(1)

    b_c[1].wait_recv()
    b_x0.wait_recv()
    for z in range(4):
        one = pr[xu, z] + got_core[1, z]
        if z < 2:
            one = one + half_x[0, z].astype(F32)
        put_x[1, z] = one.astype(BF16)
    b_x2 = ring.copy("x+", put_x.at[1], got_x.at[0])
    b_c[2].wait_recv()
    b_x1.wait_recv()
    for z in range(4):
        one = pr[xd, z] + got_core[2, z]
        if z >= 2:
            one = one + half_x[1, z - 2].astype(F32)
        put_x[2, z] = one.astype(BF16)
    b_x3 = ring.copy("x-", put_x.at[2], got_x.at[1])

    pass_far(3)
    pass_plain(0)
    pass_plain(2)
    pass_near(0)
    pass_near(2)
    pass_other(2)
    pass_plain(1)
    pass_plain(3)
    pass_near(1)
    pass_near(3)
    pass_other(3)

    b_c[3].wait_recv()
    b_x2.wait_recv()
    b_x3.wait_recv()
    for z in range(4):
        u[z] = pr[x, z] + got_core[3, z] + got_x[0, z].astype(F32) + got_x[1, z].astype(F32)
    put_z[0] = u[zf].astype(BF16)
    rlo, rhi = pl.ds(0, RHALF), pl.ds(RHALF, DP - RHALF)
    b_z0 = ring.copy("zh+", put_z.at[0, rlo], half_z.at[rlo])
    b_z1 = ring.copy("zh-", put_z.at[0, rhi], half_z.at[rhi])
    b_z0.wait_recv()
    put_z[1, 0:RHALF] = (u[zu, 0:RHALF] + half_z[0:RHALF].astype(F32)).astype(BF16)
    put_z[1, RHALF:DP] = u[zu, RHALF:DP].astype(BF16)
    b_z2 = ring.copy("zh+", put_z.at[1], got_z.at[0])
    b_z1.wait_recv()
    put_z[2, 0:RHALF] = u[zd, 0:RHALF].astype(BF16)
    put_z[2, RHALF:DP] = (u[zd, RHALF:DP] + half_z[RHALF:DP].astype(F32)).astype(BF16)
    b_z3 = ring.copy("zh-", put_z.at[2], got_z.at[1])

    for c in range(4):
        for got in (qz, q_u, q_d):
            got[c].wait_recv()

    def col_sum(start, size):
        at = pl.ds(start, size)
        return (
            pc_ref[wanted[MINE], at].astype(F32) + got_c[3, at].astype(F32)
            + got_c[4, at].astype(F32) + got_c[5, at].astype(F32)
        )

    shift = 32 * y
    back = (L - shift) % L
    lane = lax.broadcasted_iota(jnp.int32, (DP, L), 1)
    sums = [col_sum(t * DP, DP) for t in range(FULL)]
    for t in range(FULL):
        oc_ref[:, t * L : (t + 1) * L] = pltpu.roll(
            jnp.where(lane < shift, sums[(t + 1) % FULL], sums[t]), back, 1
        )
    tail = col_sum(FULL * DP, QR)
    for q in range(4):
        part = pltpu.roll(tail, L - 32 * q, 1) if q else tail
        rows = min(QR, DP - q * QR)
        oc_ref[q * QR : q * QR + rows, FULL * L :] = part[:rows]

    b_z2.wait_recv()
    b_z3.wait_recv()
    or_ref[...] = u[zh] + got_z[0].astype(F32) + got_z[1].astype(F32)
    ring.finish()


def reduce(pc, pr):
    return pl.pallas_call(
        reduce_kernel,
        out_shape=(
            pltpu.VMEM((DP, (FULL + 1) * L), F32),
            pltpu.VMEM((DP, L), F32),
        ),
        in_specs=[IN_VMEM] * 2,
        out_specs=(IN_VMEM,) * 2,
        scratch_shapes=[
            pltpu.VMEM((6, PACK, L), BF16),
            pltpu.VMEM((PACK, L), BF16),
            pltpu.VMEM((3, PACK, L), BF16),
            pltpu.VMEM((4, 4, DP, L), F32),
            pltpu.VMEM((2, 4, DP, L), BF16),
            pltpu.VMEM((3, 4, DP, L), BF16),
            pltpu.VMEM((2, 2, DP, L), BF16),
            pltpu.VMEM((DP, L), BF16),
            pltpu.VMEM((2, DP, L), BF16),
            pltpu.VMEM((3, DP, L), BF16),
            pltpu.VMEM((4, DP, L), F32),
            pltpu.SemaphoreType.DMA((COPIES,)),
            pltpu.SemaphoreType.DMA((COPIES,)),
        ],
        compiler_params=pltpu.CompilerParams(
            collective_id=1, has_side_effects=True, vmem_limit_bytes=20 * MIB
        ),
        name="reduce",
    )(pc, pr)


def outputs_kernel(oc_ref, or_ref, row_ref, row_bias_ref, col_ref, col_bias_ref):
    col_ref[...] = oc_ref[:D, :SHARD]
    col_bias_ref[...] = oc_ref[D + 1, :SHARD]
    row_ref[...] = or_ref[:D]
    row_bias_ref[...] = or_ref[D]


def outputs(oc, orow):
    return pl.pallas_call(
        outputs_kernel,
        out_shape=(
            jax.ShapeDtypeStruct((D, L), F32),
            jax.ShapeDtypeStruct((L,), F32),
            jax.ShapeDtypeStruct((D, SHARD), F32),
            jax.ShapeDtypeStruct((SHARD,), F32),
        ),
        in_specs=[IN_VMEM] * 2,
        out_specs=(IN_VMEM,) * 4,
        compiler_params=pltpu.CompilerParams(vmem_limit_bytes=8 * MIB),
        name="outputs",
    )(oc, orow)


def body(row_vecs, row_bias, col_vecs, col_bias, row_block, col_block, counts, block_totals):
    gc, gr, rn, counts = gather(
        col_vecs.T, col_bias, row_vecs.T, row_bias, counts.reshape(CAP, L, L)
    )
    pc, pr = blocks(
        block_totals, row_block, col_block, counts, gc,
        gr.reshape(ROW_TILES, DP, L), rn.reshape(ROW_TILES, L, DP),
    )
    grad_rows, grad_row_bias, grad_cols, grad_col_bias = outputs(*reduce(pc, pr.reshape(2, 4, 4, DP, L)))
    return grad_rows.T, grad_row_bias, grad_cols.T, grad_col_bias


def solution(mesh):
    placed = (
        P(("row", "col"), None),
        P(("row", "col")),
        P(("col", "row"), None),
        P(("col", "row")),
        P("row", "col", None),
        P("row", "col", None),
        P("row", "col", None, None, None),
        P(),
    )
    return jax.shard_map(
        body,
        mesh=mesh,
        in_specs=placed,
        out_specs=(
            P(("row", "col"), None),
            P(("row", "col")),
            P(("col", "row"), None),
            P(("col", "row")),
        ),
        check_vma=False,
    )
```

```python
import jax
import jax.numpy as jnp
from jax import lax
from jax.experimental import pallas as pl
from jax.experimental.pallas import tpu as pltpu
from jax.sharding import PartitionSpec as P

MESH = pl.DeviceIdType.MESH
IN_HBM = pl.BlockSpec(memory_space=pltpu.HBM)
IN_VMEM = pl.BlockSpec(memory_space=pltpu.VMEM)
IN_SMEM = pl.BlockSpec(memory_space=pltpu.SMEM)
F32, BF16 = jnp.float32, jnp.bfloat16

D = 300
DP = 304
L = 128
SHARD = 800
FULL = SHARD // L
REST = SHARD - FULL * L
QR = 80
PACK = FULL * DP + QR
CUTS = (0, 480, 960, 1440, PACK)
RHALF = 160
SHARDS = 8
ROW_TILES = 32
COL_TILES = 50
QUAD = COL_TILES // 2
CAP = 128
TILES = SHARDS * PACK + 8 * DP
GROUP = 16
DEEP = 256
MIB = 1024 * 1024


def chunk(c):
    return pl.ds(CUTS[c], CUTS[c + 1] - CUTS[c])


def place():
    row, col = lax.axis_index("row"), lax.axis_index("col")
    y, zl = row % 4, row // 4
    core, x, zh = col % 2, (col // 2) % 4, col // 8
    return y, zl, core, x, zh


def row_of(y, zl):
    return zl * 4 + y


def col_of(core, x, zh):
    return (zh * 4 + x) * 2 + core


class Ring:
    def __init__(self, send, recv):
        self.send, self.recv = send, recv
        self.y, self.zl, self.core, self.x, self.zh = place()
        y, zl, core, x, zh = self.y, self.zl, self.core, self.x, self.zh
        row, col = row_of(y, zl), col_of(core, x, zh)
        self.near = {
            "y+": (row_of((y + 1) % 4, zl), col),
            "y-": (row_of((y + 3) % 4, zl), col),
            "zl": (row_of(y, 1 - zl), col),
            "x+": (row, col_of(core, (x + 1) % 4, zh)),
            "x-": (row, col_of(core, (x + 3) % 4, zh)),
            "zh+": (row, col_of(core, x, (zh + 1) % 4)),
            "zh-": (row, col_of(core, x, (zh + 3) % 4)),
            "core": (row, col_of(1 - core, x, zh)),
        }
        self.started = []

    def greet(self):
        barrier = pltpu.get_barrier_semaphore()
        for row, col in self.near.values():
            pl.semaphore_signal(barrier, inc=1, device_id={"row": row, "col": col}, device_id_type=MESH)
        return barrier

    def meet(self, barrier):
        pl.semaphore_wait(barrier, len(self.near))

    def copy(self, to, src, dst):
        row, col = self.near[to]
        k = len(self.started)
        out = pltpu.make_async_remote_copy(
            src_ref=src,
            dst_ref=dst,
            send_sem=self.send.at[k],
            recv_sem=self.recv.at[k],
            device_id={"row": row, "col": col},
            device_id_type=MESH,
        )
        out.start()
        self.started.append(out)
        return out

    def finish(self):
        for out in self.started:
            out.wait_send()


COPIES = 48


def gather_kernel(cv_hbm, cb_hbm, rv_hbm, rb_hbm, counts_hbm, gc, gr, rn, counts, acc_c, acc_r,
                  cv_ref, cb_ref, rv_ref, rb_ref, wc, last, send, recv, local):
    pairs = ((rv_hbm, rv_ref), (rb_hbm, rb_ref), (cv_hbm, cv_ref), (cb_hbm, cb_ref), (counts_hbm, counts))
    loads = [pltpu.make_async_copy(src, dst, local.at[1 + k]) for k, (src, dst) in enumerate(pairs)]
    for load in loads:
        load.start()
    ring = Ring(send, recv)
    y, zl, core, x, zh = ring.y, ring.zl, ring.core, ring.x, ring.zh
    barrier = ring.greet()

    for load in loads[:2]:
        load.wait()
    last[0:12, 0:L] = rv_ref[288:D].astype(F32)
    last[12:13, 0:L] = rb_ref[...].astype(F32).reshape(1, L)
    last[13:14, 0:L] = jnp.ones((1, L), F32)
    last[14:16, 0:L] = jnp.zeros((2, L), F32)
    gr[core, x, zh, 0:288] = rv_ref[0:288]
    gr[core, x, zh, 288:DP] = last[0:16, 0:L].astype(BF16)

    for load in loads[2:4]:
        load.wait()
    last[0:12, 0:SHARD] = cv_ref[288:D].astype(F32)
    last[12:13] = jnp.ones((1, (FULL + 1) * L), F32)
    last[13:14, 0:SHARD] = cb_ref[...].astype(F32).reshape(1, SHARD)
    last[14:16] = jnp.zeros((2, (FULL + 1) * L), F32)
    shift = 32 * y
    lane = lax.broadcasted_iota(jnp.int32, (DP, L), 1)

    def turned(t):
        part = jnp.concatenate(
            [cv_ref[0:288, t * L : (t + 1) * L].astype(F32), last[0:16, t * L : (t + 1) * L]], axis=0
        )
        return pltpu.roll(part, shift, 1)

    before = first = turned(0)
    for t in range(1, FULL):
        part = turned(t)
        wc[t * DP : (t + 1) * DP] = jnp.where(lane < shift, before, part).astype(BF16)
        before = part
    wc[0:DP] = jnp.where(lane < shift, before, first).astype(BF16)
    part = jnp.concatenate(
        [cv_ref[0:288, FULL * L : SHARD].astype(F32), last[0:16, FULL * L : SHARD], jnp.zeros((4 * QR - DP, REST), F32)],
        axis=0,
    )
    part = jnp.concatenate([part, jnp.zeros((4 * QR, L - REST), F32)], axis=1)
    tail = part[:QR]
    for q in range(1, 4):
        tail = tail + pltpu.roll(part[q * QR : (q + 1) * QR], 32 * q, 1)
    wc[FULL * DP : PACK] = tail.astype(BF16)

    mine, other = row_of(y, zl), row_of(y, 1 - zl)
    up, down, far = row_of((y + 1) % 4, zl), row_of((y + 3) % 4, zl), row_of((y + 2) % 4, zl)
    xu, xd, xf = (x + 1) % 4, (x + 3) % 4, (x + 2) % 4
    own_c = pltpu.make_async_copy(wc, gc.at[pl.ds(mine * PACK, PACK)], local.at[0])
    own_c.start()

    def turn(c, xx):
        @pl.loop(0, 4)
        def _(z):
            rn[c, xx, z] = gr[c, xx, z].astype(F32).T.astype(BF16)

    def part_of(shard, c):
        return gc.at[pl.ds(pl.multiple_of(shard * PACK + CUTS[c], 16), CUTS[c + 1] - CUTS[c])]

    def own(to, c):
        return ring.copy(to, wc.at[chunk(c)], part_of(mine, c))

    def pass_on(to, shard, c):
        return ring.copy(to, part_of(shard, c), part_of(shard, c))

    def rows(to, *at):
        return ring.copy(to, gr.at[at], gr.at[at])

    zu, zd, zf = (zh + 1) % 4, (zh + 3) % 4, (zh + 2) % 4
    ring.meet(barrier)
    r_zu = rows("zh+", core, x, zh)
    r_zd = rows("zh-", core, x, zh)
    x_u, x_d, x_f = {}, {}, {}
    x_u["own"], x_d["own"] = rows("x+", core, x, zh), rows("x-", core, x, zh)
    c_u, c_d, c_z = {}, {}, {}
    for a, b in ((0, 2), (1, 3)):
        c_u[a], c_d[b] = own("y+", a), own("y-", b)
        c_z[a] = own("zl", a)

    f_u, f_d, f_z, o_u, o_d = {}, {}, {}, {}, {}
    c_u[0].wait_recv()
    f_u[0] = pass_on("y+", down, 0)
    c_d[2].wait_recv()
    f_d[2] = pass_on("y-", up, 2)
    c_u[2], c_d[0] = own("y+", 2), own("y-", 0)
    c_z[2] = own("zl", 2)

    r_zu.wait_recv()
    r_fu = rows("zh+", core, x, zd, pl.ds(0, RHALF))
    x_u["zd"], x_d["zd"] = rows("x+", core, x, zd), rows("x-", core, x, zd)
    r_zd.wait_recv()
    r_fd = rows("zh-", core, x, zu, pl.ds(RHALF, DP - RHALF))
    x_u["zu"], x_d["zu"] = rows("x+", core, x, zu), rows("x-", core, x, zu)

    c_u[1].wait_recv()
    f_u[1] = pass_on("y+", down, 1)
    c_d[3].wait_recv()
    f_d[3] = pass_on("y-", up, 3)
    c_u[3], c_d[1] = own("y+", 3), own("y-", 1)
    c_z[3] = own("zl", 3)

    x_u["own"].wait_recv()
    x_f["own"] = rows("x+", core, xd, zh)

    f_u[0].wait_recv()
    f_z[0] = pass_on("zl", far, 0)
    f_d[2].wait_recv()
    f_z[2] = pass_on("zl", far, 2)

    r_fu.wait_recv()
    r_fd.wait_recv()
    x_u["zf"], x_d["zf"] = rows("x+", core, x, zf), rows("x-", core, x, zf)
    x_d["zd"].wait_recv()
    x_f["zd"] = rows("x-", core, xu, zd)
    x_u["zu"].wait_recv()
    x_f["zu"] = rows("x+", core, xd, zu)
    c_z[0].wait_recv()
    o_u[0], o_d[0] = pass_on("y+", other, 0), pass_on("y-", other, 0)

    f_u[1].wait_recv()
    f_z[1] = pass_on("zl", far, 1)
    f_d[3].wait_recv()
    f_z[3] = pass_on("zl", far, 3)
    k_own = rows("core", core, x)
    for c in (1, 2):
        c_z[c].wait_recv()
        o_u[c], o_d[c] = pass_on("y+", other, c), pass_on("y-", other, c)

    x_d["zf"].wait_recv()
    x_f["zf"] = rows("x-", core, xu, zf)
    for one in (x_d["own"], x_d["zu"]):
        one.wait_recv()
    k_up = rows("core", core, xu)
    for one in (x_u["zd"], x_u["zf"]):
        one.wait_recv()
    k_down = rows("core", core, xd)
    c_z[3].wait_recv()
    o_u[3], o_d[3] = pass_on("y+", other, 3), pass_on("y-", other, 3)

    @pl.loop(0, COL_TILES)
    def _(i):
        acc_c[i] = jnp.zeros((DP, L), F32)

    @pl.loop(0, ROW_TILES)
    def _(i):
        acc_r[i] = jnp.zeros((DP, L), F32)

    turn(core, x)
    for one in x_f.values():
        one.wait_recv()
    k_far = rows("core", core, xf)
    for xx in (xd, xu, xf):
        turn(core, xx)
    for got, xx in ((k_own, x), (k_up, xu), (k_down, xd), (k_far, xf)):
        got.wait_recv()
        turn(1 - core, xx)

    for got in (c_u[2], c_u[3], c_d[0], c_d[1]):
        got.wait_recv()
    own_c.wait()
    merge_tiles(gc, zl)
    for c in range(4):
        for got in (o_u[c], o_d[c], f_z[c]):
            got.wait_recv()
    merge_tiles(gc, 1 - zl)
    ring.finish()
    loads[4].wait()


def gather(cv, cb, rv, rb, counts):
    return pl.pallas_call(
        gather_kernel,
        out_shape=(
            pltpu.VMEM((TILES, L), BF16),
            pltpu.VMEM((2, 4, 4, DP, L), BF16),
            pltpu.VMEM((2, 4, 4, L, DP), BF16),
            pltpu.VMEM((CAP, L, L), jnp.int32),
            pltpu.VMEM((COL_TILES, DP, L), F32),
            pltpu.VMEM((ROW_TILES, DP, L), F32),
        ),
        in_specs=[IN_HBM] * 5,
        out_specs=(IN_VMEM,) * 6,
        scratch_shapes=[
            pltpu.VMEM((D, SHARD), BF16),
            pltpu.VMEM((SHARD,), BF16),
            pltpu.VMEM((D, L), BF16),
            pltpu.VMEM((L,), BF16),
            pltpu.VMEM((PACK, L), BF16),
            pltpu.VMEM((16, (FULL + 1) * L), F32),
            pltpu.SemaphoreType.DMA((COPIES,)),
            pltpu.SemaphoreType.DMA((COPIES,)),
            pltpu.SemaphoreType.DMA((6,)),
        ],
        compiler_params=pltpu.CompilerParams(
            collective_id=0, has_side_effects=True, vmem_limit_bytes=8 * MIB
        ),
        name="gather",
    )(*(pltpu.with_memory_space_constraint(a, pltpu.HBM) for a in (cv, cb, rv, rb, counts)))


def merge_tiles(ct, quad):
    lane = lax.broadcasted_iota(jnp.int32, (DP, L), 1)

    def rows_at(n, size):
        return pl.ds(pl.multiple_of(n, 16), size)

    def first(k):
        return ct[rows_at((quad * 4 + k) * PACK, DP)].astype(F32)

    for k in range(4):
        part = ct[rows_at((quad * 4 + k) * PACK + FULL * DP, QR)].astype(F32)
        turns = [(32 * k - 32 * q) % L for q in range(4)]
        tile = jnp.concatenate([pltpu.roll(part, n, 1) if n else part for n in turns], axis=0)[:DP]
        if k:
            tile = jnp.where(lane < 32 * k, first(k), tile)
        if k < 3:
            tile = jnp.where(lane < 32 * (k + 1), tile, first(k + 1))
        ct[rows_at(SHARDS * PACK + (quad * 4 + k) * DP, DP)] = tile.astype(BF16)


def tile_at(b):
    quad, j = b // QUAD, b % QUAD
    k, t = j // FULL, j % FULL
    shared = (k > 0) & (t == 0)
    return jnp.where(shared, SHARDS * PACK + (quad * 4 + k - 1) * DP, (quad * 4 + k) * PACK + t * DP)


def pack_shard(tiles, s):
    k = s % 4
    base = (SHARD * s) // L
    lane = lax.broadcasted_iota(jnp.int32, (DP, L), 1)
    lane_q = lax.broadcasted_iota(jnp.int32, (QR, L), 1)
    after = tiles[base + FULL]
    head = tiles[base]
    if k:
        head = jnp.where(lane < 32 * k, after, head)
    parts = [(0, head)] + [(t * DP, tiles[base + t]) for t in range(1, FULL)]
    after = jnp.concatenate([after, jnp.zeros((4 * QR - DP, L), F32)], axis=0)
    tail = None
    for q in range(4):
        n = (32 * q - 32 * k) % L
        part = after[q * QR : (q + 1) * QR]
        part = pltpu.roll(part, n, 1) if n else part
        tail = part if q == 0 else jnp.where(lane_q < 32 * q, tail, part)
    return parts + [(FULL * DP, tail)]


LOG2_100 = 6.643856189774724
LN2 = 0.6931471805599453


def blocks_kernel(total_ref, rid_ref, cid_ref, counts, ct, rt, rn, zero_c, zero_r, pc, acc_r, acc_c):
    row, col = lax.axis_index("row"), lax.axis_index("col")
    total = total_ref[row, col]
    groups = (total + GROUP - 1) // GROUP

    @pl.loop(0, groups)
    def _(g):
        terms, rids, cids, tiles = [], [], [], []
        for k in range(GROUP):
            n = g * GROUP + k
            rid, cid = rid_ref[0, 0, n], cid_ref[0, 0, n]
            rid = rid % 2 * 16 + rid // 2 % 4 * 4 + rid // 8
            rids.append(rid)
            cids.append(cid)
            at = pl.multiple_of(tile_at(cid), 16)
            tiles.append(pl.ds(at, DP))
            scores = jnp.dot(rn[rid, :, :DEEP], ct[pl.ds(at, DEEP)], preferred_element_type=F32)
            scores += jnp.dot(rn[rid, :, DEEP:], ct[pl.ds(at + DEEP, DP - DEEP)], preferred_element_type=F32)
            x = counts[n]
            least = jnp.where(n < total, 0, jnp.int32(2**31 - 1))
            log2x = jnp.log2(jnp.maximum(x.astype(F32), 1.0))
            weight2 = jnp.exp2(jnp.minimum(0.75 * log2x + (1.0 - 0.75 * LOG2_100), 1.0))
            term = weight2 * (scores - LN2 * log2x)
            terms.append(jnp.where(x > least, term, 0.0).astype(BF16))
        for k in range(GROUP):
            term, none = terms[k], jnp.zeros((L, L), BF16)
            both = jnp.concatenate(
                [jnp.concatenate([term, none], axis=1), jnp.concatenate([none, term.T], axis=1)], axis=0
            )
            vecs = jnp.concatenate([rt[rids[k]], ct[tiles[k]]], axis=1)
            grads = jnp.dot(vecs, both, preferred_element_type=F32)
            acc_c[cids[k]] += grads[:, :L]
            acc_r[rids[k]] += grads[:, L:]

    for s in range(SHARDS):
        for at, part in pack_shard(acc_c, s):
            pc[s, at : at + part.shape[0]] = part.astype(BF16)


def blocks(totals, rid, cid, counts, gc, gr, rn, acc_c, acc_r):
    return pl.pallas_call(
        blocks_kernel,
        out_shape=(
            pltpu.VMEM((SHARDS, PACK, L), BF16),
            pltpu.VMEM((ROW_TILES, DP, L), F32),
            pltpu.VMEM((COL_TILES, DP, L), F32),
        ),
        in_specs=[IN_SMEM] * 3 + [IN_VMEM] * 6,
        out_specs=(IN_VMEM,) * 3,
        input_output_aliases={7: 2, 8: 1},
        compiler_params=pltpu.CompilerParams(vmem_limit_bytes=8 * MIB),
        name="blocks",
    )(totals, rid, cid, counts, gc, gr, rn, acc_c, acc_r)


def reduce_kernel(pc_ref, pr_ref, oc_ref, or_ref,
                  got_c, half_c, put_c, got_core, got_x, put_x, half_x, half_z, got_z, put_z, u,
                  send, recv):
    ring = Ring(send, recv)
    y, zl, core, x, zh = ring.y, ring.zl, ring.core, ring.x, ring.zh
    zo = 1 - zl
    barrier = ring.greet()
    up, down, far = (y + 1) % 4, (y + 3) % 4, (y + 2) % 4
    xu, xd, xf = (x + 1) % 4, (x + 3) % 4, (x + 2) % 4
    zu, zd, zf = (zh + 1) % 4, (zh + 3) % 4, (zh + 2) % 4
    FAR, OTHER, UP, DOWN, MINE = range(5)
    wanted = (row_of(far, zl), row_of(y, zo), row_of(up, zl), row_of(down, zl), row_of(y, zl))
    pr = pr_ref.at[core]
    ring.meet(barrier)

    def raw(to, y_to, c, k):
        return ring.copy(to, pc_ref.at[row_of(y_to, zo), chunk(c)], got_c.at[k, chunk(c)])

    def put(to, k, c, dst):
        return ring.copy(to, put_c.at[k, chunk(c)], dst.at[chunk(c)])

    def total(k, c, *more):
        at = chunk(c)
        out = pc_ref[wanted[k], at].astype(F32)
        for one in more:
            out = out + one[at].astype(F32)
        return out

    a_z, a_u, a_d = {}, {}, {}
    for c in (0, 1):
        a_z[2 * c] = raw("zl", far, 2 * c, 0)
        a_u[c], a_d[c] = raw("y+", up, c, 1), raw("y-", down, c, 2)
    for c in (1, 3):
        a_z[c] = raw("zl", far, c, 0)
    b_c = [ring.copy("core", pr_ref.at[1 - core, w], got_core.at[k]) for k, w in enumerate((xf, xu, xd, x))]

    q2 = {}

    def pass_far(c):
        a_z[c].wait_recv()
        put_c[0, chunk(c)] = total(FAR, c, got_c.at[0]).astype(BF16)
        q2[c] = put("y+" if c < 2 else "y-", 0, c, half_c)

    qz = {}

    def pass_other(c):
        a_u[c].wait_recv()
        a_d[c].wait_recv()
        put_c[1, chunk(c)] = total(OTHER, c, got_c.at[1], got_c.at[2]).astype(BF16)
        qz[c] = put("zl", 1, c, got_c.at[3])

    q_u, q_d = {}, {}

    def pass_near(c):
        q2[c].wait_recv()
        if c < 2:
            put_c[2, chunk(c)] = total(UP, c, half_c).astype(BF16)
            q_u[c] = put("y+", 2, c, got_c.at[4])
        else:
            put_c[2, chunk(c)] = total(DOWN, c, half_c).astype(BF16)
            q_d[c] = put("y-", 2, c, got_c.at[5])

    def pass_plain(c):
        if c < 2:
            q_d[c] = ring.copy("y-", pc_ref.at[wanted[DOWN], chunk(c)], got_c.at[5, chunk(c)])
        else:
            q_u[c] = ring.copy("y+", pc_ref.at[wanted[UP], chunk(c)], got_c.at[4, chunk(c)])

    x_far, x_up, x_down = {}, {}, {}

    def row_far():
        b_c[0].wait_recv()
        for k, z in enumerate((zf, zu, zd, zh)):
            put_x[0, z] = (pr[xf, z] + got_core[0, z]).astype(BF16)
            x_far[k] = ring.copy("x-" if k % 2 else "x+", put_x.at[0, z], half_x.at[z])

    def row_near(to, k):
        z = (zf, zu, zd, zh)[k]
        up_side = to == "x+"
        one = pr[xu, z] + got_core[1, z] if up_side else pr[xd, z] + got_core[2, z]
        if up_side == (k % 2 == 0):
            x_far[k].wait_recv()
            one = one + half_x[z].astype(F32)
        slot, side = (1, 0) if up_side else (2, 1)
        put_x[slot, z] = one.astype(BF16)
        (x_up if up_side else x_down)[k] = ring.copy(to, put_x.at[slot, z], got_x.at[side, z])

    def row_sum(k):
        z = (zf, zu, zd, zh)[k]
        x_up[k].wait_recv()
        x_down[k].wait_recv()
        return pr[x, z] + got_core[3, z] + got_x[0, z].astype(F32) + got_x[1, z].astype(F32)

    pass_far(0)
    a_u[2], a_d[2] = raw("y+", up, 2, 1), raw("y-", down, 2, 2)
    row_far()
    pass_far(2)
    a_u[3], a_d[3] = raw("y+", up, 3, 1), raw("y-", down, 3, 2)
    b_c[1].wait_recv()
    b_c[2].wait_recv()
    row_near("x-", 0)
    row_near("x+", 1)
    pass_other(0)
    pass_far(1)
    row_near("x+", 0)
    row_near("x-", 1)
    row_near("x-", 2)
    row_near("x+", 3)
    pass_other(1)
    pass_far(3)
    pass_plain(0)
    pass_plain(2)
    row_near("x+", 2)
    row_near("x-", 3)
    pass_near(0)
    pass_near(2)

    b_c[3].wait_recv()
    rlo, rhi = pl.ds(0, RHALF), pl.ds(RHALF, DP - RHALF)
    put_z[0] = row_sum(0).astype(BF16)
    b_z0 = ring.copy("zh+", put_z.at[0, rlo], half_z.at[rlo])
    b_z1 = ring.copy("zh-", put_z.at[0, rhi], half_z.at[rhi])
    pass_other(2)
    pass_plain(1)
    pass_plain(3)
    u[0] = row_sum(1)
    u[1] = row_sum(2)
    pass_near(1)
    pass_near(3)
    b_z0.wait_recv()
    put_z[1, 0:RHALF] = (u[0, 0:RHALF] + half_z[0:RHALF].astype(F32)).astype(BF16)
    put_z[1, RHALF:DP] = u[0, RHALF:DP].astype(BF16)
    b_z2 = ring.copy("zh+", put_z.at[1], got_z.at[0])
    b_z1.wait_recv()
    put_z[2, 0:RHALF] = u[1, 0:RHALF].astype(BF16)
    put_z[2, RHALF:DP] = (u[1, RHALF:DP] + half_z[RHALF:DP].astype(F32)).astype(BF16)
    b_z3 = ring.copy("zh-", put_z.at[2], got_z.at[1])
    pass_other(3)
    u[0] = row_sum(3)

    for c in range(4):
        for got in (qz, q_u, q_d):
            got[c].wait_recv()

    def col_sum(start, size):
        at = pl.ds(start, size)
        return (
            pc_ref[wanted[MINE], at].astype(F32) + got_c[3, at].astype(F32)
            + got_c[4, at].astype(F32) + got_c[5, at].astype(F32)
        )

    shift = 32 * y
    back = (L - shift) % L
    lane = lax.broadcasted_iota(jnp.int32, (DP, L), 1)
    sums = [col_sum(t * DP, DP) for t in range(FULL)]
    for t in range(FULL):
        oc_ref[:, t * L : (t + 1) * L] = pltpu.roll(
            jnp.where(lane < shift, sums[(t + 1) % FULL], sums[t]), back, 1
        )
    tail = col_sum(FULL * DP, QR)
    for q in range(4):
        part = pltpu.roll(tail, L - 32 * q, 1) if q else tail
        rows = min(QR, DP - q * QR)
        oc_ref[q * QR : q * QR + rows, FULL * L :] = part[:rows]

    b_z2.wait_recv()
    b_z3.wait_recv()
    or_ref[...] = u[0] + got_z[0].astype(F32) + got_z[1].astype(F32)
    ring.finish()


def reduce(pc, pr):
    return pl.pallas_call(
        reduce_kernel,
        out_shape=(
            pltpu.VMEM((DP, (FULL + 1) * L), F32),
            pltpu.VMEM((DP, L), F32),
        ),
        in_specs=[IN_VMEM] * 2,
        out_specs=(IN_VMEM,) * 2,
        scratch_shapes=[
            pltpu.VMEM((6, PACK, L), BF16),
            pltpu.VMEM((PACK, L), BF16),
            pltpu.VMEM((3, PACK, L), BF16),
            pltpu.VMEM((4, 4, DP, L), F32),
            pltpu.VMEM((2, 4, DP, L), BF16),
            pltpu.VMEM((3, 4, DP, L), BF16),
            pltpu.VMEM((4, DP, L), BF16),
            pltpu.VMEM((DP, L), BF16),
            pltpu.VMEM((2, DP, L), BF16),
            pltpu.VMEM((3, DP, L), BF16),
            pltpu.VMEM((2, DP, L), F32),
            pltpu.SemaphoreType.DMA((COPIES,)),
            pltpu.SemaphoreType.DMA((COPIES,)),
        ],
        compiler_params=pltpu.CompilerParams(
            collective_id=1, has_side_effects=True, vmem_limit_bytes=20 * MIB
        ),
        name="reduce",
    )(pc, pr)


def outputs_kernel(oc_ref, or_ref, row_ref, row_bias_ref, col_ref, col_bias_ref):
    col_ref[...] = oc_ref[:D, :SHARD]
    col_bias_ref[...] = oc_ref[D + 1, :SHARD]
    row_ref[...] = or_ref[:D]
    row_bias_ref[...] = or_ref[D]


def outputs(oc, orow):
    return pl.pallas_call(
        outputs_kernel,
        out_shape=(
            jax.ShapeDtypeStruct((D, L), F32),
            jax.ShapeDtypeStruct((L,), F32),
            jax.ShapeDtypeStruct((D, SHARD), F32),
            jax.ShapeDtypeStruct((SHARD,), F32),
        ),
        in_specs=[IN_VMEM] * 2,
        out_specs=(IN_VMEM,) * 4,
        compiler_params=pltpu.CompilerParams(vmem_limit_bytes=8 * MIB),
        name="outputs",
    )(oc, orow)


def body(row_vecs, row_bias, col_vecs, col_bias, row_block, col_block, counts, block_totals):
    gc, gr, rn, counts, acc_c, acc_r = gather(
        col_vecs.T, col_bias, row_vecs.T, row_bias, counts.reshape(CAP, L, L)
    )
    pc, pr, _ = blocks(
        block_totals, row_block, col_block, counts, gc,
        gr.reshape(ROW_TILES, DP, L), rn.reshape(ROW_TILES, L, DP), acc_c, acc_r,
    )
    grad_rows, grad_row_bias, grad_cols, grad_col_bias = outputs(*reduce(pc, pr.reshape(2, 4, 4, DP, L)))
    return grad_rows.T, grad_row_bias, grad_cols.T, grad_col_bias


def solution(mesh):
    placed = (
        P(("row", "col"), None),
        P(("row", "col")),
        P(("col", "row"), None),
        P(("col", "row")),
        P("row", "col", None),
        P("row", "col", None),
        P("row", "col", None, None, None),
        P(),
    )
    return jax.shard_map(
        body,
        mesh=mesh,
        in_specs=placed,
        out_specs=(
            P(("row", "col"), None),
            P(("row", "col")),
            P(("col", "row"), None),
            P(("col", "row")),
        ),
        check_vma=False,
    )
```

```python
import jax
import jax.numpy as jnp
from jax import lax
from jax.experimental import pallas as pl
from jax.experimental.pallas import tpu as pltpu
from jax.sharding import PartitionSpec as P

MESH = pl.DeviceIdType.MESH
IN_HBM = pl.BlockSpec(memory_space=pltpu.HBM)
IN_VMEM = pl.BlockSpec(memory_space=pltpu.VMEM)
IN_SMEM = pl.BlockSpec(memory_space=pltpu.SMEM)
F32, BF16 = jnp.float32, jnp.bfloat16

D = 300
DP = 304
L = 128
SHARD = 800
FULL = SHARD // L
REST = SHARD - FULL * L
QR = 80
PACK = FULL * DP + QR
CUTS = (0, 480, 960, 1440, PACK)
RHALF = 160
SHARDS = 8
ROW_TILES = 32
COL_TILES = 50
QUAD = COL_TILES // 2
CAP = 128
TILES = SHARDS * PACK + 8 * DP
GROUP = 32
BEHIND = 4
DEEP = 256
MIB = 1024 * 1024


def chunk(c):
    return pl.ds(CUTS[c], CUTS[c + 1] - CUTS[c])


def place():
    row, col = lax.axis_index("row"), lax.axis_index("col")
    y, zl = row % 4, row // 4
    core, x, zh = col % 2, (col // 2) % 4, col // 8
    return y, zl, core, x, zh


def row_of(y, zl):
    return zl * 4 + y


def col_of(core, x, zh):
    return (zh * 4 + x) * 2 + core


class Ring:
    def __init__(self, send, recv):
        self.send, self.recv = send, recv
        self.y, self.zl, self.core, self.x, self.zh = place()
        y, zl, core, x, zh = self.y, self.zl, self.core, self.x, self.zh
        row, col = row_of(y, zl), col_of(core, x, zh)
        self.near = {
            "y+": (row_of((y + 1) % 4, zl), col),
            "y-": (row_of((y + 3) % 4, zl), col),
            "zl": (row_of(y, 1 - zl), col),
            "x+": (row, col_of(core, (x + 1) % 4, zh)),
            "x-": (row, col_of(core, (x + 3) % 4, zh)),
            "zh+": (row, col_of(core, x, (zh + 1) % 4)),
            "zh-": (row, col_of(core, x, (zh + 3) % 4)),
            "core": (row, col_of(1 - core, x, zh)),
        }
        self.started = []

    def greet(self):
        barrier = pltpu.get_barrier_semaphore()
        for row, col in self.near.values():
            pl.semaphore_signal(barrier, inc=1, device_id={"row": row, "col": col}, device_id_type=MESH)
        return barrier

    def meet(self, barrier):
        pl.semaphore_wait(barrier, len(self.near))

    def copy(self, to, src, dst):
        row, col = self.near[to]
        k = len(self.started)
        out = pltpu.make_async_remote_copy(
            src_ref=src,
            dst_ref=dst,
            send_sem=self.send.at[k],
            recv_sem=self.recv.at[k],
            device_id={"row": row, "col": col},
            device_id_type=MESH,
        )
        out.start()
        self.started.append(out)
        return out

    def finish(self):
        for out in self.started:
            out.wait_send()


COPIES = 48


def gather_kernel(cv_hbm, cb_hbm, rv_hbm, rb_hbm, counts_hbm, gc, gr, rn, counts, acc_c, acc_r,
                  cv_ref, cb_ref, rv_ref, rb_ref, wc, last, send, recv, local):
    pairs = ((rv_hbm, rv_ref), (rb_hbm, rb_ref), (cv_hbm, cv_ref), (cb_hbm, cb_ref), (counts_hbm, counts))
    loads = [pltpu.make_async_copy(src, dst, local.at[1 + k]) for k, (src, dst) in enumerate(pairs)]
    for load in loads:
        load.start()
    ring = Ring(send, recv)
    y, zl, core, x, zh = ring.y, ring.zl, ring.core, ring.x, ring.zh
    barrier = ring.greet()

    for load in loads[:2]:
        load.wait()
    last[0:12, 0:L] = rv_ref[288:D].astype(F32)
    last[12:13, 0:L] = rb_ref[...].astype(F32).reshape(1, L)
    last[13:14, 0:L] = jnp.ones((1, L), F32)
    last[14:16, 0:L] = jnp.zeros((2, L), F32)
    gr[core, x, zh, 0:288] = rv_ref[0:288]
    gr[core, x, zh, 288:DP] = last[0:16, 0:L].astype(BF16)

    for load in loads[2:4]:
        load.wait()
    last[0:12, 0:SHARD] = cv_ref[288:D].astype(F32)
    last[12:13] = jnp.ones((1, (FULL + 1) * L), F32)
    last[13:14, 0:SHARD] = cb_ref[...].astype(F32).reshape(1, SHARD)
    last[14:16] = jnp.zeros((2, (FULL + 1) * L), F32)
    shift = 32 * y
    lane = lax.broadcasted_iota(jnp.int32, (DP, L), 1)

    def turned(t):
        part = jnp.concatenate(
            [cv_ref[0:288, t * L : (t + 1) * L].astype(F32), last[0:16, t * L : (t + 1) * L]], axis=0
        )
        return pltpu.roll(part, shift, 1)

    before = first = turned(0)
    for t in range(1, FULL):
        part = turned(t)
        wc[t * DP : (t + 1) * DP] = jnp.where(lane < shift, before, part).astype(BF16)
        before = part
    wc[0:DP] = jnp.where(lane < shift, before, first).astype(BF16)
    part = jnp.concatenate(
        [cv_ref[0:288, FULL * L : SHARD].astype(F32), last[0:16, FULL * L : SHARD], jnp.zeros((4 * QR - DP, REST), F32)],
        axis=0,
    )
    part = jnp.concatenate([part, jnp.zeros((4 * QR, L - REST), F32)], axis=1)
    tail = part[:QR]
    for q in range(1, 4):
        tail = tail + pltpu.roll(part[q * QR : (q + 1) * QR], 32 * q, 1)
    wc[FULL * DP : PACK] = tail.astype(BF16)

    mine, other = row_of(y, zl), row_of(y, 1 - zl)
    up, down, far = row_of((y + 1) % 4, zl), row_of((y + 3) % 4, zl), row_of((y + 2) % 4, zl)
    xu, xd, xf = (x + 1) % 4, (x + 3) % 4, (x + 2) % 4
    own_c = pltpu.make_async_copy(wc, gc.at[pl.ds(mine * PACK, PACK)], local.at[0])
    own_c.start()

    def turn(c, xx):
        @pl.loop(0, 4)
        def _(z):
            rn[c, xx, z] = gr[c, xx, z].astype(F32).T.astype(BF16)

    def part_of(shard, c):
        return gc.at[pl.ds(pl.multiple_of(shard * PACK + CUTS[c], 16), CUTS[c + 1] - CUTS[c])]

    def own(to, c):
        return ring.copy(to, wc.at[chunk(c)], part_of(mine, c))

    def pass_on(to, shard, c):
        return ring.copy(to, part_of(shard, c), part_of(shard, c))

    def rows(to, *at):
        return ring.copy(to, gr.at[at], gr.at[at])

    zu, zd, zf = (zh + 1) % 4, (zh + 3) % 4, (zh + 2) % 4
    ring.meet(barrier)
    r_zu = rows("zh+", core, x, zh)
    r_zd = rows("zh-", core, x, zh)
    x_u, x_d, x_f = {}, {}, {}
    x_u["own"], x_d["own"] = rows("x+", core, x, zh), rows("x-", core, x, zh)
    c_u, c_d, c_z = {}, {}, {}
    for a, b in ((0, 2), (1, 3)):
        c_u[a], c_d[b] = own("y+", a), own("y-", b)
        c_z[a] = own("zl", a)

    f_u, f_d, f_z, o_u, o_d = {}, {}, {}, {}, {}
    c_u[0].wait_recv()
    f_u[0] = pass_on("y+", down, 0)
    c_d[2].wait_recv()
    f_d[2] = pass_on("y-", up, 2)
    c_u[2], c_d[0] = own("y+", 2), own("y-", 0)
    c_z[2] = own("zl", 2)

    r_zu.wait_recv()
    r_fu = rows("zh+", core, x, zd, pl.ds(0, RHALF))
    x_u["zd"], x_d["zd"] = rows("x+", core, x, zd), rows("x-", core, x, zd)
    r_zd.wait_recv()
    r_fd = rows("zh-", core, x, zu, pl.ds(RHALF, DP - RHALF))
    x_u["zu"], x_d["zu"] = rows("x+", core, x, zu), rows("x-", core, x, zu)

    c_u[1].wait_recv()
    f_u[1] = pass_on("y+", down, 1)
    c_d[3].wait_recv()
    f_d[3] = pass_on("y-", up, 3)
    c_u[3], c_d[1] = own("y+", 3), own("y-", 1)
    c_z[3] = own("zl", 3)

    x_u["own"].wait_recv()
    x_f["own"] = rows("x+", core, xd, zh)

    f_u[0].wait_recv()
    f_z[0] = pass_on("zl", far, 0)
    f_d[2].wait_recv()
    f_z[2] = pass_on("zl", far, 2)

    r_fu.wait_recv()
    r_fd.wait_recv()
    x_u["zf"], x_d["zf"] = rows("x+", core, x, zf), rows("x-", core, x, zf)
    x_d["zd"].wait_recv()
    x_f["zd"] = rows("x-", core, xu, zd)
    x_u["zu"].wait_recv()
    x_f["zu"] = rows("x+", core, xd, zu)
    c_z[0].wait_recv()
    o_u[0], o_d[0] = pass_on("y+", other, 0), pass_on("y-", other, 0)

    f_u[1].wait_recv()
    f_z[1] = pass_on("zl", far, 1)
    f_d[3].wait_recv()
    f_z[3] = pass_on("zl", far, 3)
    k_own = rows("core", core, x)
    for c in (1, 2):
        c_z[c].wait_recv()
        o_u[c], o_d[c] = pass_on("y+", other, c), pass_on("y-", other, c)

    x_d["zf"].wait_recv()
    x_f["zf"] = rows("x-", core, xu, zf)
    for one in (x_d["own"], x_d["zu"]):
        one.wait_recv()
    k_up = rows("core", core, xu)
    for one in (x_u["zd"], x_u["zf"]):
        one.wait_recv()
    k_down = rows("core", core, xd)
    c_z[3].wait_recv()
    o_u[3], o_d[3] = pass_on("y+", other, 3), pass_on("y-", other, 3)

    @pl.loop(0, COL_TILES)
    def _(i):
        acc_c[i] = jnp.zeros((DP, L), F32)

    @pl.loop(0, ROW_TILES)
    def _(i):
        acc_r[i] = jnp.zeros((DP, L), F32)

    turn(core, x)
    for one in x_f.values():
        one.wait_recv()
    k_far = rows("core", core, xf)
    for xx in (xd, xu, xf):
        turn(core, xx)
    for got, xx in ((k_own, x), (k_up, xu), (k_down, xd), (k_far, xf)):
        got.wait_recv()
        turn(1 - core, xx)

    for got in (c_u[2], c_u[3], c_d[0], c_d[1]):
        got.wait_recv()
    own_c.wait()
    merge_tiles(gc, zl)
    for c in range(4):
        for got in (o_u[c], o_d[c], f_z[c]):
            got.wait_recv()
    merge_tiles(gc, 1 - zl)
    ring.finish()
    loads[4].wait()


def gather(cv, cb, rv, rb, counts):
    return pl.pallas_call(
        gather_kernel,
        out_shape=(
            pltpu.VMEM((TILES, L), BF16),
            pltpu.VMEM((2, 4, 4, DP, L), BF16),
            pltpu.VMEM((2, 4, 4, L, DP), BF16),
            pltpu.VMEM((CAP, L, L), jnp.int32),
            pltpu.VMEM((COL_TILES, DP, L), F32),
            pltpu.VMEM((ROW_TILES, DP, L), F32),
        ),
        in_specs=[IN_HBM] * 5,
        out_specs=(IN_VMEM,) * 6,
        scratch_shapes=[
            pltpu.VMEM((D, SHARD), BF16),
            pltpu.VMEM((SHARD,), BF16),
            pltpu.VMEM((D, L), BF16),
            pltpu.VMEM((L,), BF16),
            pltpu.VMEM((PACK, L), BF16),
            pltpu.VMEM((16, (FULL + 1) * L), F32),
            pltpu.SemaphoreType.DMA((COPIES,)),
            pltpu.SemaphoreType.DMA((COPIES,)),
            pltpu.SemaphoreType.DMA((6,)),
        ],
        compiler_params=pltpu.CompilerParams(
            collective_id=0, has_side_effects=True, vmem_limit_bytes=8 * MIB
        ),
        name="gather",
    )(*(pltpu.with_memory_space_constraint(a, pltpu.HBM) for a in (cv, cb, rv, rb, counts)))


def merge_tiles(ct, quad):
    lane = lax.broadcasted_iota(jnp.int32, (DP, L), 1)

    def rows_at(n, size):
        return pl.ds(pl.multiple_of(n, 16), size)

    def first(k):
        return ct[rows_at((quad * 4 + k) * PACK, DP)].astype(F32)

    for k in range(4):
        part = ct[rows_at((quad * 4 + k) * PACK + FULL * DP, QR)].astype(F32)
        turns = [(32 * k - 32 * q) % L for q in range(4)]
        tile = jnp.concatenate([pltpu.roll(part, n, 1) if n else part for n in turns], axis=0)[:DP]
        if k:
            tile = jnp.where(lane < 32 * k, first(k), tile)
        if k < 3:
            tile = jnp.where(lane < 32 * (k + 1), tile, first(k + 1))
        ct[rows_at(SHARDS * PACK + (quad * 4 + k) * DP, DP)] = tile.astype(BF16)


def tile_at(b):
    quad = (b >= QUAD).astype(jnp.int32)
    j = b - QUAD * quad
    k = (j * 43) >> 8
    t = j - FULL * k
    shared = (k > 0) & (t == 0)
    at = jnp.where(shared, SHARDS * PACK + (quad * 4 + k - 1) * DP, (quad * 4 + k) * PACK + t * DP)
    return pl.multiple_of(at, 16)


def pack_shard(tiles, y, zl, packed, slot):
    base, shift = QUAD * zl + FULL * y, 32 * y
    lane = lax.broadcasted_iota(jnp.int32, (DP, L), 1)
    lane_q = lax.broadcasted_iota(jnp.int32, (QR, L), 1)
    after = tiles[base + FULL]
    packed[slot, 0:DP] = jnp.where(lane < shift, after, tiles[base]).astype(BF16)
    for t in range(1, FULL):
        packed[slot, t * DP : (t + 1) * DP] = tiles[base + t].astype(BF16)
    after = jnp.concatenate([after, jnp.zeros((4 * QR - DP, L), F32)], axis=0)
    tail = None
    for q in range(4):
        part = pltpu.roll(after[q * QR : (q + 1) * QR], (32 * q + L - shift) % L, 1)
        tail = part if q == 0 else jnp.where(lane_q < 32 * q, tail, part)
    packed[slot, FULL * DP : PACK] = tail.astype(BF16)


LOG2_100 = 6.643856189774724
LN2 = 0.6931471805599453


def blocks_kernel(total_ref, rid_ref, cid_ref, counts, ct, rt, rn, zero_c, zero_r, acc_c, acc_r):
    row, col = lax.axis_index("row"), lax.axis_index("col")
    total = total_ref[row, col]
    groups = (total + GROUP - 1) // GROUP

    @pl.loop(0, groups)
    def _(g):
        slots = []

        def terms_of(n):
            rid, cid = rid_ref[0, 0, n], cid_ref[0, 0, n]
            rid = ((rid & 1) << 4) + (((rid >> 1) & 3) << 2) + (rid >> 3)
            at = tile_at(cid)
            scores = jnp.dot(rn[rid, :, :DEEP], ct[pl.ds(at, DEEP)], preferred_element_type=F32)
            scores += jnp.dot(rn[rid, :, DEEP:], ct[pl.ds(at + DEEP, DP - DEEP)], preferred_element_type=F32)
            x = counts[n]
            least = jnp.where(n < total, 0, jnp.int32(2**31 - 1))
            log2x = jnp.log2(jnp.maximum(x.astype(F32), 1.0))
            weight2 = jnp.exp2(jnp.minimum(0.75 * log2x + (1.0 - 0.75 * LOG2_100), 1.0))
            term = weight2 * (scores - LN2 * log2x)
            return rid, cid, at, jnp.where(x > least, term, 0.0).astype(BF16)

        def add(rid, cid, at, term):
            none = jnp.zeros((L, L), BF16)
            both = jnp.concatenate(
                [jnp.concatenate([term, none], axis=1), jnp.concatenate([none, term.T], axis=1)], axis=0
            )
            vecs = jnp.concatenate([rt[rid], ct[pl.ds(at, DP)]], axis=1)
            grads = jnp.dot(vecs, both, preferred_element_type=F32)
            acc_c[cid] += grads[:, :L]
            acc_r[rid] += grads[:, L:]

        for k in range(GROUP + BEHIND):
            if k < GROUP:
                slots.append(terms_of(g * GROUP + k))
            if k >= BEHIND:
                add(*slots[k - BEHIND])


def blocks(totals, rid, cid, counts, gc, gr, rn, acc_c, acc_r):
    return pl.pallas_call(
        blocks_kernel,
        out_shape=(
            pltpu.VMEM((COL_TILES, DP, L), F32),
            pltpu.VMEM((ROW_TILES, DP, L), F32),
        ),
        in_specs=[IN_SMEM] * 3 + [IN_VMEM] * 6,
        out_specs=(IN_VMEM,) * 2,
        input_output_aliases={7: 0, 8: 1},
        compiler_params=pltpu.CompilerParams(vmem_limit_bytes=8 * MIB),
        name="blocks",
    )(totals, rid, cid, counts, gc, gr, rn, acc_c, acc_r)


def reduce_kernel(acc_ref, pr_ref, oc_ref, or_ref,
                  pc, fin, got_c, half_c, put_c, got_core, got_x, put_x, half_x, half_z, got_z, put_z, u,
                  send, recv):
    ring = Ring(send, recv)
    y, zl, core, x, zh = ring.y, ring.zl, ring.core, ring.x, ring.zh
    zo = 1 - zl
    barrier = ring.greet()
    up, down, far = (y + 1) % 4, (y + 3) % 4, (y + 2) % 4
    xu, xd, xf = (x + 1) % 4, (x + 3) % 4, (x + 2) % 4
    zu, zd, zf = (zh + 1) % 4, (zh + 3) % 4, (zh + 2) % 4
    FAR_O, UP_O, DOWN_O, FAR, OTHER, UP, DOWN, MINE = range(SHARDS)
    wanted = ((far, zo), (up, zo), (down, zo), (far, zl), (y, zo), (up, zl), (down, zl), (y, zl))

    def pack(*slots):
        for k in slots:
            pack_shard(acc_ref, *wanted[k], pc, k)

    pack(FAR_O, UP_O, DOWN_O)
    pr = pr_ref.at[core]
    ring.meet(barrier)

    def raw(to, k, c, got):
        return ring.copy(to, pc.at[k, chunk(c)], got_c.at[got, chunk(c)])

    def put(to, k, c, dst):
        return ring.copy(to, put_c.at[k, chunk(c)], dst.at[chunk(c)])

    def total(k, c, *more):
        at = chunk(c)
        out = pc[k, at].astype(F32)
        for one in more:
            out = out + one[at].astype(F32)
        return out

    a_z, a_u, a_d = {}, {}, {}
    for c in (0, 1):
        a_z[2 * c] = raw("zl", FAR_O, 2 * c, 0)
        a_u[c], a_d[c] = raw("y+", UP_O, c, 1), raw("y-", DOWN_O, c, 2)
    for c in (1, 3):
        a_z[c] = raw("zl", FAR_O, c, 0)
    b_c = [ring.copy("core", pr_ref.at[1 - core, w], got_core.at[k]) for k, w in enumerate((xf, xu, xd, x))]

    q2 = {}

    def pass_far(c):
        a_z[c].wait_recv()
        put_c[0, chunk(c)] = total(FAR, c, got_c.at[0]).astype(BF16)
        q2[c] = put("y+" if c < 2 else "y-", 0, c, half_c)

    qz = {}

    def pass_other(c):
        a_u[c].wait_recv()
        a_d[c].wait_recv()
        put_c[1, chunk(c)] = total(OTHER, c, got_c.at[1], got_c.at[2]).astype(BF16)
        qz[c] = put("zl", 1, c, got_c.at[3])

    q_u, q_d = {}, {}

    def pass_near(c):
        q2[c].wait_recv()
        if c < 2:
            put_c[2, chunk(c)] = total(UP, c, half_c).astype(BF16)
            q_u[c] = put("y+", 2, c, got_c.at[4])
        else:
            put_c[2, chunk(c)] = total(DOWN, c, half_c).astype(BF16)
            q_d[c] = put("y-", 2, c, got_c.at[5])

    def pass_plain(c):
        if c < 2:
            q_d[c] = ring.copy("y-", pc.at[DOWN, chunk(c)], got_c.at[5, chunk(c)])
        else:
            q_u[c] = ring.copy("y+", pc.at[UP, chunk(c)], got_c.at[4, chunk(c)])

    x_far, x_up, x_down = {}, {}, {}

    def row_far():
        b_c[0].wait_recv()
        for k, z in enumerate((zf, zu, zd, zh)):
            put_x[0, z] = (pr[xf, z] + got_core[0, z]).astype(BF16)
            x_far[k] = ring.copy("x-" if k % 2 else "x+", put_x.at[0, z], half_x.at[z])

    def row_near(to, k):
        z = (zf, zu, zd, zh)[k]
        up_side = to == "x+"
        one = pr[xu, z] + got_core[1, z] if up_side else pr[xd, z] + got_core[2, z]
        if up_side == (k % 2 == 0):
            x_far[k].wait_recv()
            one = one + half_x[z].astype(F32)
        slot, side = (1, 0) if up_side else (2, 1)
        put_x[slot, z] = one.astype(BF16)
        (x_up if up_side else x_down)[k] = ring.copy(to, put_x.at[slot, z], got_x.at[side, z])

    def row_sum(k):
        z = (zf, zu, zd, zh)[k]
        x_up[k].wait_recv()
        x_down[k].wait_recv()
        return pr[x, z] + got_core[3, z] + got_x[0, z].astype(F32) + got_x[1, z].astype(F32)

    pack(FAR)
    pass_far(0)
    a_u[2], a_d[2] = raw("y+", UP_O, 2, 1), raw("y-", DOWN_O, 2, 2)
    row_far()
    pass_far(2)
    a_u[3], a_d[3] = raw("y+", UP_O, 3, 1), raw("y-", DOWN_O, 3, 2)
    b_c[1].wait_recv()
    b_c[2].wait_recv()
    row_near("x-", 0)
    row_near("x+", 1)
    pack(OTHER)
    pass_other(0)
    pass_far(1)
    row_near("x+", 0)
    row_near("x-", 1)
    row_near("x-", 2)
    row_near("x+", 3)
    pass_other(1)
    pass_far(3)
    pack(UP, DOWN)
    pass_plain(0)
    pass_plain(2)
    row_near("x+", 2)
    row_near("x-", 3)
    pass_near(0)
    pass_near(2)

    b_c[3].wait_recv()
    rlo, rhi = pl.ds(0, RHALF), pl.ds(RHALF, DP - RHALF)
    put_z[0] = row_sum(0).astype(BF16)
    b_z0 = ring.copy("zh+", put_z.at[0, rlo], half_z.at[rlo])
    b_z1 = ring.copy("zh-", put_z.at[0, rhi], half_z.at[rhi])
    pass_other(2)
    pass_plain(1)
    pass_plain(3)
    u[0] = row_sum(1)
    u[1] = row_sum(2)
    pass_near(1)
    pass_near(3)
    b_z0.wait_recv()
    put_z[1, 0:RHALF] = (u[0, 0:RHALF] + half_z[0:RHALF].astype(F32)).astype(BF16)
    put_z[1, RHALF:DP] = u[0, RHALF:DP].astype(BF16)
    b_z2 = ring.copy("zh+", put_z.at[1], got_z.at[0])
    b_z1.wait_recv()
    put_z[2, 0:RHALF] = u[1, 0:RHALF].astype(BF16)
    put_z[2, RHALF:DP] = (u[1, RHALF:DP] + half_z[RHALF:DP].astype(F32)).astype(BF16)
    b_z3 = ring.copy("zh-", put_z.at[2], got_z.at[1])
    pass_other(3)
    u[0] = row_sum(3)
    pack(MINE)

    for c in range(4):
        for got in (qz, q_u, q_d):
            got[c].wait_recv()
        fin[chunk(c)] = total(MINE, c, got_c.at[3], got_c.at[4], got_c.at[5])

    shift = 32 * y
    back = (L - shift) % L
    lane = lax.broadcasted_iota(jnp.int32, (DP, L), 1)
    sums = [fin[t * DP : (t + 1) * DP] for t in range(FULL)]
    for t in range(FULL):
        oc_ref[:, t * L : (t + 1) * L] = pltpu.roll(
            jnp.where(lane < shift, sums[(t + 1) % FULL], sums[t]), back, 1
        )
    tail = fin[FULL * DP : PACK]
    for q in range(4):
        part = pltpu.roll(tail, L - 32 * q, 1) if q else tail
        rows = min(QR, DP - q * QR)
        oc_ref[q * QR : q * QR + rows, FULL * L :] = part[:rows]

    b_z2.wait_recv()
    b_z3.wait_recv()
    or_ref[...] = u[0] + got_z[0].astype(F32) + got_z[1].astype(F32)
    ring.finish()


def reduce(acc_c, pr):
    return pl.pallas_call(
        reduce_kernel,
        out_shape=(
            pltpu.VMEM((DP, (FULL + 1) * L), F32),
            pltpu.VMEM((DP, L), F32),
        ),
        in_specs=[IN_VMEM] * 2,
        out_specs=(IN_VMEM,) * 2,
        scratch_shapes=[
            pltpu.VMEM((SHARDS, PACK, L), BF16),
            pltpu.VMEM((PACK, L), F32),
            pltpu.VMEM((6, PACK, L), BF16),
            pltpu.VMEM((PACK, L), BF16),
            pltpu.VMEM((3, PACK, L), BF16),
            pltpu.VMEM((4, 4, DP, L), F32),
            pltpu.VMEM((2, 4, DP, L), BF16),
            pltpu.VMEM((3, 4, DP, L), BF16),
            pltpu.VMEM((4, DP, L), BF16),
            pltpu.VMEM((DP, L), BF16),
            pltpu.VMEM((2, DP, L), BF16),
            pltpu.VMEM((3, DP, L), BF16),
            pltpu.VMEM((2, DP, L), F32),
            pltpu.SemaphoreType.DMA((COPIES,)),
            pltpu.SemaphoreType.DMA((COPIES,)),
        ],
        compiler_params=pltpu.CompilerParams(
            collective_id=1, has_side_effects=True, vmem_limit_bytes=20 * MIB
        ),
        name="reduce",
    )(acc_c, pr)


def outputs_kernel(oc_ref, or_ref, row_ref, row_bias_ref, col_ref, col_bias_ref):
    col_ref[...] = oc_ref[:D, :SHARD]
    col_bias_ref[...] = oc_ref[D + 1, :SHARD]
    row_ref[...] = or_ref[:D]
    row_bias_ref[...] = or_ref[D]


def outputs(oc, orow):
    return pl.pallas_call(
        outputs_kernel,
        out_shape=(
            jax.ShapeDtypeStruct((D, L), F32),
            jax.ShapeDtypeStruct((L,), F32),
            jax.ShapeDtypeStruct((D, SHARD), F32),
            jax.ShapeDtypeStruct((SHARD,), F32),
        ),
        in_specs=[IN_VMEM] * 2,
        out_specs=(IN_VMEM,) * 4,
        compiler_params=pltpu.CompilerParams(vmem_limit_bytes=8 * MIB),
        name="outputs",
    )(oc, orow)


def body(row_vecs, row_bias, col_vecs, col_bias, row_block, col_block, counts, block_totals):
    gc, gr, rn, counts, acc_c, acc_r = gather(
        col_vecs.T, col_bias, row_vecs.T, row_bias, counts.reshape(CAP, L, L)
    )
    acc_c, acc_r = blocks(
        block_totals, row_block, col_block, counts, gc,
        gr.reshape(ROW_TILES, DP, L), rn.reshape(ROW_TILES, L, DP), acc_c, acc_r,
    )
    grad_rows, grad_row_bias, grad_cols, grad_col_bias = outputs(*reduce(acc_c, acc_r.reshape(2, 4, 4, DP, L)))
    return grad_rows.T, grad_row_bias, grad_cols.T, grad_col_bias


def solution(mesh):
    placed = (
        P(("row", "col"), None),
        P(("row", "col")),
        P(("col", "row"), None),
        P(("col", "row")),
        P("row", "col", None),
        P("row", "col", None),
        P("row", "col", None, None, None),
        P(),
    )
    return jax.shard_map(
        body,
        mesh=mesh,
        in_specs=placed,
        out_specs=(
            P(("row", "col"), None),
            P(("row", "col")),
            P(("col", "row"), None),
            P(("col", "row")),
        ),
        check_vma=False,
    )
```

```python
import jax
import jax.numpy as jnp
from jax import lax
from jax.experimental import pallas as pl
from jax.experimental.pallas import tpu as pltpu
from jax.sharding import PartitionSpec as P

MESH = pl.DeviceIdType.MESH
IN_HBM = pl.BlockSpec(memory_space=pltpu.HBM)
IN_VMEM = pl.BlockSpec(memory_space=pltpu.VMEM)
IN_SMEM = pl.BlockSpec(memory_space=pltpu.SMEM)
F32, BF16 = jnp.float32, jnp.bfloat16

D = 300
DP = 304
L = 128
SHARD = 800
FULL = SHARD // L
REST = SHARD - FULL * L
QR = 80
PACK = FULL * DP + QR
CUTS = (0, 480, 960, 1440, PACK)
RHALF = 160
SHARDS = 8
ROW_TILES = 32
COL_TILES = 50
QUAD = COL_TILES // 2
CAP = 128
TILES = SHARDS * PACK + 8 * DP
GROUP = 32
BEHIND = 4
DEEP = 256
MIB = 1024 * 1024


def chunk(c):
    return pl.ds(CUTS[c], CUTS[c + 1] - CUTS[c])


def place():
    row, col = lax.axis_index("row"), lax.axis_index("col")
    y, zl = row % 4, row // 4
    core, x, zh = col % 2, (col // 2) % 4, col // 8
    return y, zl, core, x, zh


def row_of(y, zl):
    return zl * 4 + y


def col_of(core, x, zh):
    return (zh * 4 + x) * 2 + core


class Ring:
    def __init__(self, send, recv):
        self.send, self.recv = send, recv
        self.y, self.zl, self.core, self.x, self.zh = place()
        y, zl, core, x, zh = self.y, self.zl, self.core, self.x, self.zh
        row, col = row_of(y, zl), col_of(core, x, zh)
        self.near = {
            "y+": (row_of((y + 1) % 4, zl), col),
            "y-": (row_of((y + 3) % 4, zl), col),
            "zl": (row_of(y, 1 - zl), col),
            "x+": (row, col_of(core, (x + 1) % 4, zh)),
            "x-": (row, col_of(core, (x + 3) % 4, zh)),
            "zh+": (row, col_of(core, x, (zh + 1) % 4)),
            "zh-": (row, col_of(core, x, (zh + 3) % 4)),
            "core": (row, col_of(1 - core, x, zh)),
        }
        self.started = []

    def greet(self):
        barrier = pltpu.get_barrier_semaphore()
        for row, col in self.near.values():
            pl.semaphore_signal(barrier, inc=1, device_id={"row": row, "col": col}, device_id_type=MESH)
        return barrier

    def meet(self, barrier):
        pl.semaphore_wait(barrier, len(self.near))

    def copy(self, to, src, dst):
        row, col = self.near[to]
        k = len(self.started)
        out = pltpu.make_async_remote_copy(
            src_ref=src,
            dst_ref=dst,
            send_sem=self.send.at[k],
            recv_sem=self.recv.at[k],
            device_id={"row": row, "col": col},
            device_id_type=MESH,
        )
        out.start()
        self.started.append(out)
        return out

    def finish(self):
        for out in self.started:
            out.wait_send()


COPIES = 48


def gather_kernel(cv_hbm, cb_hbm, rv_hbm, rb_hbm, counts_hbm, gc, gr, rn, counts, acc_c, acc_r,
                  cv_ref, cb_ref, rv_ref, rb_ref, wc, last, send, recv, local):
    pairs = ((rv_hbm, rv_ref), (rb_hbm, rb_ref), (cv_hbm, cv_ref), (cb_hbm, cb_ref), (counts_hbm, counts))
    loads = [pltpu.make_async_copy(src, dst, local.at[1 + k]) for k, (src, dst) in enumerate(pairs)]
    for load in loads[:4]:
        load.start()
    ring = Ring(send, recv)
    y, zl, core, x, zh = ring.y, ring.zl, ring.core, ring.x, ring.zh
    barrier = ring.greet()

    for load in loads[:2]:
        load.wait()
    last[0:12, 0:L] = rv_ref[288:D].astype(F32)
    last[12:13, 0:L] = rb_ref[...].astype(F32).reshape(1, L)
    last[13:14, 0:L] = jnp.ones((1, L), F32)
    last[14:16, 0:L] = jnp.zeros((2, L), F32)
    gr[core, x, zh, 0:288] = rv_ref[0:288]
    gr[core, x, zh, 288:DP] = last[0:16, 0:L].astype(BF16)

    for load in loads[2:4]:
        load.wait()
    last[0:12, 0:SHARD] = cv_ref[288:D].astype(F32)
    last[12:13] = jnp.ones((1, (FULL + 1) * L), F32)
    last[13:14, 0:SHARD] = cb_ref[...].astype(F32).reshape(1, SHARD)
    last[14:16] = jnp.zeros((2, (FULL + 1) * L), F32)
    shift = 32 * y
    lane = lax.broadcasted_iota(jnp.int32, (DP, L), 1)

    def turned(t):
        part = jnp.concatenate(
            [cv_ref[0:288, t * L : (t + 1) * L].astype(F32), last[0:16, t * L : (t + 1) * L]], axis=0
        )
        return pltpu.roll(part, shift, 1)

    before = first = turned(0)
    for t in range(1, FULL):
        part = turned(t)
        wc[t * DP : (t + 1) * DP] = jnp.where(lane < shift, before, part).astype(BF16)
        before = part
    wc[0:DP] = jnp.where(lane < shift, before, first).astype(BF16)
    part = jnp.concatenate(
        [cv_ref[0:288, FULL * L : SHARD].astype(F32), last[0:16, FULL * L : SHARD], jnp.zeros((4 * QR - DP, REST), F32)],
        axis=0,
    )
    part = jnp.concatenate([part, jnp.zeros((4 * QR, L - REST), F32)], axis=1)
    tail = part[:QR]
    for q in range(1, 4):
        tail = tail + pltpu.roll(part[q * QR : (q + 1) * QR], 32 * q, 1)
    wc[FULL * DP : PACK] = tail.astype(BF16)

    mine, other = row_of(y, zl), row_of(y, 1 - zl)
    up, down, far = row_of((y + 1) % 4, zl), row_of((y + 3) % 4, zl), row_of((y + 2) % 4, zl)
    xu, xd, xf = (x + 1) % 4, (x + 3) % 4, (x + 2) % 4
    own_c = pltpu.make_async_copy(wc, gc.at[pl.ds(mine * PACK, PACK)], local.at[0])
    own_c.start()

    def turn(c, xx):
        @pl.loop(0, 4)
        def _(z):
            rn[c, xx, z] = gr[c, xx, z].astype(F32).T.astype(BF16)

    def part_of(shard, c):
        return gc.at[pl.ds(pl.multiple_of(shard * PACK + CUTS[c], 16), CUTS[c + 1] - CUTS[c])]

    def own(to, c):
        return ring.copy(to, wc.at[chunk(c)], part_of(mine, c))

    def pass_on(to, shard, c):
        return ring.copy(to, part_of(shard, c), part_of(shard, c))

    def rows(to, *at):
        return ring.copy(to, gr.at[at], gr.at[at])

    zu, zd, zf = (zh + 1) % 4, (zh + 3) % 4, (zh + 2) % 4
    ring.meet(barrier)
    r_zu = rows("zh+", core, x, zh)
    r_zd = rows("zh-", core, x, zh)
    x_u, x_d, x_f = {}, {}, {}
    x_u["own"], x_d["own"] = rows("x+", core, x, zh), rows("x-", core, x, zh)
    c_u, c_d, c_z = {}, {}, {}
    for a, b in ((0, 2), (1, 3)):
        c_u[a], c_d[b] = own("y+", a), own("y-", b)
        c_z[a] = own("zl", a)

    f_u, f_d, f_z, o_u, o_d = {}, {}, {}, {}, {}
    c_u[0].wait_recv()
    f_u[0] = pass_on("y+", down, 0)
    c_d[2].wait_recv()
    f_d[2] = pass_on("y-", up, 2)
    c_u[2], c_d[0] = own("y+", 2), own("y-", 0)
    c_z[2] = own("zl", 2)
    loads[4].start()

    r_zu.wait_recv()
    r_fu = rows("zh+", core, x, zd, pl.ds(0, RHALF))
    x_u["zd"], x_d["zd"] = rows("x+", core, x, zd), rows("x-", core, x, zd)
    r_zd.wait_recv()
    r_fd = rows("zh-", core, x, zu, pl.ds(RHALF, DP - RHALF))
    x_u["zu"], x_d["zu"] = rows("x+", core, x, zu), rows("x-", core, x, zu)

    c_u[1].wait_recv()
    f_u[1] = pass_on("y+", down, 1)
    c_d[3].wait_recv()
    f_d[3] = pass_on("y-", up, 3)
    c_u[3], c_d[1] = own("y+", 3), own("y-", 1)
    c_z[3] = own("zl", 3)

    x_u["own"].wait_recv()
    x_f["own"] = rows("x+", core, xd, zh)

    f_u[0].wait_recv()
    f_z[0] = pass_on("zl", far, 0)
    f_d[2].wait_recv()
    f_z[2] = pass_on("zl", far, 2)

    r_fu.wait_recv()
    r_fd.wait_recv()
    x_u["zf"], x_d["zf"] = rows("x+", core, x, zf), rows("x-", core, x, zf)
    x_d["zd"].wait_recv()
    x_f["zd"] = rows("x-", core, xu, zd)
    x_u["zu"].wait_recv()
    x_f["zu"] = rows("x+", core, xd, zu)
    c_z[0].wait_recv()
    o_u[0], o_d[0] = pass_on("y+", other, 0), pass_on("y-", other, 0)

    f_u[1].wait_recv()
    f_z[1] = pass_on("zl", far, 1)
    f_d[3].wait_recv()
    f_z[3] = pass_on("zl", far, 3)
    k_own = rows("core", core, x)
    for c in (1, 2):
        c_z[c].wait_recv()
        o_u[c], o_d[c] = pass_on("y+", other, c), pass_on("y-", other, c)

    x_d["zf"].wait_recv()
    x_f["zf"] = rows("x-", core, xu, zf)
    for one in (x_d["own"], x_d["zu"]):
        one.wait_recv()
    k_up = rows("core", core, xu)
    for one in (x_u["zd"], x_u["zf"]):
        one.wait_recv()
    k_down = rows("core", core, xd)
    c_z[3].wait_recv()
    o_u[3], o_d[3] = pass_on("y+", other, 3), pass_on("y-", other, 3)

    @pl.loop(0, COL_TILES)
    def _(i):
        acc_c[i] = jnp.zeros((DP, L), F32)

    @pl.loop(0, ROW_TILES)
    def _(i):
        acc_r[i] = jnp.zeros((DP, L), F32)

    turn(core, x)
    for one in x_f.values():
        one.wait_recv()
    k_far = rows("core", core, xf)
    for xx in (xd, xu, xf):
        turn(core, xx)
    for got, xx in ((k_own, x), (k_up, xu), (k_down, xd), (k_far, xf)):
        got.wait_recv()
        turn(1 - core, xx)

    for got in (c_u[2], c_u[3], c_d[0], c_d[1]):
        got.wait_recv()
    own_c.wait()
    merge_tiles(gc, zl)
    for c in range(4):
        for got in (o_u[c], o_d[c], f_z[c]):
            got.wait_recv()
    merge_tiles(gc, 1 - zl)
    ring.finish()
    loads[4].wait()


def gather(cv, cb, rv, rb, counts):
    return pl.pallas_call(
        gather_kernel,
        out_shape=(
            pltpu.VMEM((TILES, L), BF16),
            pltpu.VMEM((2, 4, 4, DP, L), BF16),
            pltpu.VMEM((2, 4, 4, L, DP), BF16),
            pltpu.VMEM((CAP, L, L), jnp.int32),
            pltpu.VMEM((COL_TILES, DP, L), F32),
            pltpu.VMEM((ROW_TILES, DP, L), F32),
        ),
        in_specs=[IN_HBM] * 5,
        out_specs=(IN_VMEM,) * 6,
        scratch_shapes=[
            pltpu.VMEM((D, SHARD), BF16),
            pltpu.VMEM((SHARD,), BF16),
            pltpu.VMEM((D, L), BF16),
            pltpu.VMEM((L,), BF16),
            pltpu.VMEM((PACK, L), BF16),
            pltpu.VMEM((16, (FULL + 1) * L), F32),
            pltpu.SemaphoreType.DMA((COPIES,)),
            pltpu.SemaphoreType.DMA((COPIES,)),
            pltpu.SemaphoreType.DMA((6,)),
        ],
        compiler_params=pltpu.CompilerParams(
            collective_id=0, has_side_effects=True, vmem_limit_bytes=8 * MIB
        ),
        name="gather",
    )(*(pltpu.with_memory_space_constraint(a, pltpu.HBM) for a in (cv, cb, rv, rb, counts)))


def merge_tiles(ct, quad):
    lane = lax.broadcasted_iota(jnp.int32, (DP, L), 1)

    def rows_at(n, size):
        return pl.ds(pl.multiple_of(n, 16), size)

    def first(k):
        return ct[rows_at((quad * 4 + k) * PACK, DP)].astype(F32)

    for k in range(4):
        part = ct[rows_at((quad * 4 + k) * PACK + FULL * DP, QR)].astype(F32)
        turns = [(32 * k - 32 * q) % L for q in range(4)]
        tile = jnp.concatenate([pltpu.roll(part, n, 1) if n else part for n in turns], axis=0)[:DP]
        if k:
            tile = jnp.where(lane < 32 * k, first(k), tile)
        if k < 3:
            tile = jnp.where(lane < 32 * (k + 1), tile, first(k + 1))
        ct[rows_at(SHARDS * PACK + (quad * 4 + k) * DP, DP)] = tile.astype(BF16)


def tile_at(b):
    quad = (b >= QUAD).astype(jnp.int32)
    j = b - QUAD * quad
    k = (j * 43) >> 8
    t = j - FULL * k
    shared = (k > 0) & (t == 0)
    at = jnp.where(shared, SHARDS * PACK + (quad * 4 + k - 1) * DP, (quad * 4 + k) * PACK + t * DP)
    return pl.multiple_of(at, 16)


def pack_shard(tiles, y, zl, packed, slot):
    base, shift = QUAD * zl + FULL * y, 32 * y
    lane = lax.broadcasted_iota(jnp.int32, (DP, L), 1)
    lane_q = lax.broadcasted_iota(jnp.int32, (QR, L), 1)
    after = tiles[base + FULL]
    packed[slot, 0:DP] = jnp.where(lane < shift, after, tiles[base]).astype(BF16)
    for t in range(1, FULL):
        packed[slot, t * DP : (t + 1) * DP] = tiles[base + t].astype(BF16)
    after = jnp.concatenate([after, jnp.zeros((4 * QR - DP, L), F32)], axis=0)
    tail = None
    for q in range(4):
        part = pltpu.roll(after[q * QR : (q + 1) * QR], (32 * q + L - shift) % L, 1)
        tail = part if q == 0 else jnp.where(lane_q < 32 * q, tail, part)
    packed[slot, FULL * DP : PACK] = tail.astype(BF16)


LOG2_100 = 6.643856189774724
LN2 = 0.6931471805599453


def blocks_kernel(total_ref, rid_ref, cid_ref, counts, ct, rt, rn, zero_c, zero_r, acc_c, acc_r):
    row, col = lax.axis_index("row"), lax.axis_index("col")
    total = total_ref[row, col]
    groups = (total + GROUP - 1) // GROUP

    @pl.loop(0, groups)
    def _(g):
        slots = []

        def terms_of(n):
            rid, cid = rid_ref[0, 0, n], cid_ref[0, 0, n]
            rid = ((rid & 1) << 4) + (((rid >> 1) & 3) << 2) + (rid >> 3)
            at = tile_at(cid)
            scores = jnp.dot(rn[rid, :, :DEEP], ct[pl.ds(at, DEEP)], preferred_element_type=F32)
            scores += jnp.dot(rn[rid, :, DEEP:], ct[pl.ds(at + DEEP, DP - DEEP)], preferred_element_type=F32)
            x = counts[n]
            least = jnp.where(n < total, 0, jnp.int32(2**31 - 1))
            log2x = jnp.log2(jnp.maximum(x.astype(F32), 1.0))
            weight2 = jnp.exp2(jnp.minimum(0.75 * log2x + (1.0 - 0.75 * LOG2_100), 1.0))
            term = weight2 * (scores - LN2 * log2x)
            return rid, cid, at, jnp.where(x > least, term, 0.0).astype(BF16)

        def add(rid, cid, at, term):
            none = jnp.zeros((L, L), BF16)
            both = jnp.concatenate(
                [jnp.concatenate([term, none], axis=1), jnp.concatenate([none, term.T], axis=1)], axis=0
            )
            vecs = jnp.concatenate([rt[rid], ct[pl.ds(at, DP)]], axis=1)
            grads = jnp.dot(vecs, both, preferred_element_type=F32)
            acc_c[cid] += grads[:, :L]
            acc_r[rid] += grads[:, L:]

        for k in range(GROUP + BEHIND):
            if k < GROUP:
                slots.append(terms_of(g * GROUP + k))
            if k >= BEHIND:
                add(*slots[k - BEHIND])


def blocks(totals, rid, cid, counts, gc, gr, rn, acc_c, acc_r):
    return pl.pallas_call(
        blocks_kernel,
        out_shape=(
            pltpu.VMEM((COL_TILES, DP, L), F32),
            pltpu.VMEM((ROW_TILES, DP, L), F32),
        ),
        in_specs=[IN_SMEM] * 3 + [IN_VMEM] * 6,
        out_specs=(IN_VMEM,) * 2,
        input_output_aliases={7: 0, 8: 1},
        compiler_params=pltpu.CompilerParams(vmem_limit_bytes=8 * MIB),
        name="blocks",
    )(totals, rid, cid, counts, gc, gr, rn, acc_c, acc_r)


def reduce_kernel(acc_ref, pr_ref, oc_ref, or_ref,
                  pc, fin, got_c, half_c, put_c, got_core, got_x, put_x, half_x, half_z, got_z, put_z, u,
                  send, recv):
    ring = Ring(send, recv)
    y, zl, core, x, zh = ring.y, ring.zl, ring.core, ring.x, ring.zh
    zo = 1 - zl
    barrier = ring.greet()
    up, down, far = (y + 1) % 4, (y + 3) % 4, (y + 2) % 4
    xu, xd, xf = (x + 1) % 4, (x + 3) % 4, (x + 2) % 4
    zu, zd, zf = (zh + 1) % 4, (zh + 3) % 4, (zh + 2) % 4
    FAR_O, UP_O, DOWN_O, FAR, OTHER, UP, DOWN, MINE = range(SHARDS)
    wanted = ((far, zo), (up, zo), (down, zo), (far, zl), (y, zo), (up, zl), (down, zl), (y, zl))

    def pack(*slots):
        for k in slots:
            pack_shard(acc_ref, *wanted[k], pc, k)

    pack(UP_O)
    pr = pr_ref.at[core]
    ring.meet(barrier)

    def raw(to, k, c, got):
        return ring.copy(to, pc.at[k, chunk(c)], got_c.at[got, chunk(c)])

    def put(to, k, c, dst):
        return ring.copy(to, put_c.at[k, chunk(c)], dst.at[chunk(c)])

    def total(k, c, *more):
        at = chunk(c)
        out = pc[k, at].astype(F32)
        for one in more:
            out = out + one[at].astype(F32)
        return out

    a_z, a_u, a_d = {}, {}, {}
    for c in (0, 1):
        a_u[c] = raw("y+", UP_O, c, 1)
    pack(FAR_O)
    for c in (0, 2):
        a_z[c] = raw("zl", FAR_O, c, 0)
    pack(DOWN_O)
    for c in (0, 1):
        a_d[c] = raw("y-", DOWN_O, c, 2)
    for c in (1, 3):
        a_z[c] = raw("zl", FAR_O, c, 0)
    b_c = [ring.copy("core", pr_ref.at[1 - core, w], got_core.at[k]) for k, w in enumerate((xf, xu, xd, x))]

    q2 = {}

    def pass_far(c):
        a_z[c].wait_recv()
        put_c[0, chunk(c)] = total(FAR, c, got_c.at[0]).astype(BF16)
        q2[c] = put("y+" if c < 2 else "y-", 0, c, half_c)

    qz = {}

    def pass_other(c):
        a_u[c].wait_recv()
        a_d[c].wait_recv()
        put_c[1, chunk(c)] = total(OTHER, c, got_c.at[1], got_c.at[2]).astype(BF16)
        qz[c] = put("zl", 1, c, got_c.at[3])

    q_u, q_d = {}, {}

    def pass_near(c):
        q2[c].wait_recv()
        if c < 2:
            put_c[2, chunk(c)] = total(UP, c, half_c).astype(BF16)
            q_u[c] = put("y+", 2, c, got_c.at[4])
        else:
            put_c[2, chunk(c)] = total(DOWN, c, half_c).astype(BF16)
            q_d[c] = put("y-", 2, c, got_c.at[5])

    def pass_plain(c):
        if c < 2:
            q_d[c] = ring.copy("y-", pc.at[DOWN, chunk(c)], got_c.at[5, chunk(c)])
        else:
            q_u[c] = ring.copy("y+", pc.at[UP, chunk(c)], got_c.at[4, chunk(c)])

    x_far, x_up, x_down = {}, {}, {}

    def row_far():
        b_c[0].wait_recv()
        for k, z in enumerate((zf, zu, zd, zh)):
            put_x[0, z] = (pr[xf, z] + got_core[0, z]).astype(BF16)
            x_far[k] = ring.copy("x-" if k % 2 else "x+", put_x.at[0, z], half_x.at[z])

    def row_near(to, k):
        z = (zf, zu, zd, zh)[k]
        up_side = to == "x+"
        one = pr[xu, z] + got_core[1, z] if up_side else pr[xd, z] + got_core[2, z]
        if up_side == (k % 2 == 0):
            x_far[k].wait_recv()
            one = one + half_x[z].astype(F32)
        slot, side = (1, 0) if up_side else (2, 1)
        put_x[slot, z] = one.astype(BF16)
        (x_up if up_side else x_down)[k] = ring.copy(to, put_x.at[slot, z], got_x.at[side, z])

    def row_sum(k):
        z = (zf, zu, zd, zh)[k]
        x_up[k].wait_recv()
        x_down[k].wait_recv()
        return pr[x, z] + got_core[3, z] + got_x[0, z].astype(F32) + got_x[1, z].astype(F32)

    pack(FAR)
    pass_far(0)
    a_u[2], a_d[2] = raw("y+", UP_O, 2, 1), raw("y-", DOWN_O, 2, 2)
    row_far()
    pass_far(2)
    a_u[3], a_d[3] = raw("y+", UP_O, 3, 1), raw("y-", DOWN_O, 3, 2)
    b_c[1].wait_recv()
    b_c[2].wait_recv()
    row_near("x-", 0)
    row_near("x+", 1)
    pack(OTHER)
    pass_other(0)
    pass_far(1)
    row_near("x+", 0)
    row_near("x-", 1)
    row_near("x-", 2)
    row_near("x+", 3)
    pass_other(1)
    pass_far(3)
    pack(UP, DOWN)
    pass_plain(0)
    pass_plain(2)
    row_near("x+", 2)
    row_near("x-", 3)
    pass_near(0)
    pass_near(2)

    b_c[3].wait_recv()
    rlo, rhi = pl.ds(0, RHALF), pl.ds(RHALF, DP - RHALF)
    put_z[0] = row_sum(0).astype(BF16)
    b_z0 = ring.copy("zh+", put_z.at[0, rlo], half_z.at[rlo])
    b_z1 = ring.copy("zh-", put_z.at[0, rhi], half_z.at[rhi])
    pass_other(2)
    pass_plain(1)
    pass_plain(3)
    u[0] = row_sum(1)
    u[1] = row_sum(2)
    pass_near(1)
    pass_near(3)
    b_z0.wait_recv()
    put_z[1, 0:RHALF] = (u[0, 0:RHALF] + half_z[0:RHALF].astype(F32)).astype(BF16)
    put_z[1, RHALF:DP] = u[0, RHALF:DP].astype(BF16)
    b_z2 = ring.copy("zh+", put_z.at[1], got_z.at[0])
    b_z1.wait_recv()
    put_z[2, 0:RHALF] = u[1, 0:RHALF].astype(BF16)
    put_z[2, RHALF:DP] = (u[1, RHALF:DP] + half_z[RHALF:DP].astype(F32)).astype(BF16)
    b_z3 = ring.copy("zh-", put_z.at[2], got_z.at[1])
    pass_other(3)
    u[0] = row_sum(3)
    pack(MINE)

    for c in range(4):
        for got in (qz, q_u, q_d):
            got[c].wait_recv()
        fin[chunk(c)] = total(MINE, c, got_c.at[3], got_c.at[4], got_c.at[5])

    shift = 32 * y
    back = (L - shift) % L
    lane = lax.broadcasted_iota(jnp.int32, (DP, L), 1)
    sums = [fin[t * DP : (t + 1) * DP] for t in range(FULL)]
    for t in range(FULL):
        oc_ref[:, t * L : (t + 1) * L] = pltpu.roll(
            jnp.where(lane < shift, sums[(t + 1) % FULL], sums[t]), back, 1
        )
    tail = fin[FULL * DP : PACK]
    for q in range(4):
        part = pltpu.roll(tail, L - 32 * q, 1) if q else tail
        rows = min(QR, DP - q * QR)
        oc_ref[q * QR : q * QR + rows, FULL * L :] = part[:rows]

    b_z2.wait_recv()
    b_z3.wait_recv()
    or_ref[...] = u[0] + got_z[0].astype(F32) + got_z[1].astype(F32)
    ring.finish()


def reduce(acc_c, pr):
    return pl.pallas_call(
        reduce_kernel,
        out_shape=(
            pltpu.VMEM((DP, (FULL + 1) * L), F32),
            pltpu.VMEM((DP, L), F32),
        ),
        in_specs=[IN_VMEM] * 2,
        out_specs=(IN_VMEM,) * 2,
        scratch_shapes=[
            pltpu.VMEM((SHARDS, PACK, L), BF16),
            pltpu.VMEM((PACK, L), F32),
            pltpu.VMEM((6, PACK, L), BF16),
            pltpu.VMEM((PACK, L), BF16),
            pltpu.VMEM((3, PACK, L), BF16),
            pltpu.VMEM((4, 4, DP, L), F32),
            pltpu.VMEM((2, 4, DP, L), BF16),
            pltpu.VMEM((3, 4, DP, L), BF16),
            pltpu.VMEM((4, DP, L), BF16),
            pltpu.VMEM((DP, L), BF16),
            pltpu.VMEM((2, DP, L), BF16),
            pltpu.VMEM((3, DP, L), BF16),
            pltpu.VMEM((2, DP, L), F32),
            pltpu.SemaphoreType.DMA((COPIES,)),
            pltpu.SemaphoreType.DMA((COPIES,)),
        ],
        compiler_params=pltpu.CompilerParams(
            collective_id=1, has_side_effects=True, vmem_limit_bytes=20 * MIB
        ),
        name="reduce",
    )(acc_c, pr)


def outputs_kernel(oc_ref, or_ref, row_ref, row_bias_ref, col_ref, col_bias_ref):
    col_ref[...] = oc_ref[:D, :SHARD]
    col_bias_ref[...] = oc_ref[D + 1, :SHARD]
    row_ref[...] = or_ref[:D]
    row_bias_ref[...] = or_ref[D]


def outputs(oc, orow):
    return pl.pallas_call(
        outputs_kernel,
        out_shape=(
            jax.ShapeDtypeStruct((D, L), F32),
            jax.ShapeDtypeStruct((L,), F32),
            jax.ShapeDtypeStruct((D, SHARD), F32),
            jax.ShapeDtypeStruct((SHARD,), F32),
        ),
        in_specs=[IN_VMEM] * 2,
        out_specs=(IN_VMEM,) * 4,
        compiler_params=pltpu.CompilerParams(vmem_limit_bytes=8 * MIB),
        name="outputs",
    )(oc, orow)


def body(row_vecs, row_bias, col_vecs, col_bias, row_block, col_block, counts, block_totals):
    gc, gr, rn, counts, acc_c, acc_r = gather(
        col_vecs.T, col_bias, row_vecs.T, row_bias, counts.reshape(CAP, L, L)
    )
    acc_c, acc_r = blocks(
        block_totals, row_block, col_block, counts, gc,
        gr.reshape(ROW_TILES, DP, L), rn.reshape(ROW_TILES, L, DP), acc_c, acc_r,
    )
    grad_rows, grad_row_bias, grad_cols, grad_col_bias = outputs(*reduce(acc_c, acc_r.reshape(2, 4, 4, DP, L)))
    return grad_rows.T, grad_row_bias, grad_cols.T, grad_col_bias


def solution(mesh):
    placed = (
        P(("row", "col"), None),
        P(("row", "col")),
        P(("col", "row"), None),
        P(("col", "row")),
        P("row", "col", None),
        P("row", "col", None),
        P("row", "col", None, None, None),
        P(),
    )
    return jax.shard_map(
        body,
        mesh=mesh,
        in_specs=placed,
        out_specs=(
            P(("row", "col"), None),
            P(("row", "col")),
            P(("col", "row"), None),
            P(("col", "row")),
        ),
        check_vma=False,
    )
```
